32 devices in a mesh: cuts: 4 (over y, x), dev: 8 (over z, core).
Axes of the slice: x: 2, y: 2, z: 4, core: 2. Of those that a mesh axis runs over, the one named last changes fastest.
Arguments:
- kv_cache: bfloat16 [256, 128, 2048], P(('cuts', 'dev')), may hold values from -6 to 6
- queries: bfloat16 [4, 8, 768, 128], P('cuts', 'dev'), may hold values from -6 to 6
- gates: bfloat16 [4, 1, 768, 1024], P('cuts', None, 'dev'), may hold values from -6 to 6
- tokens: bfloat16 [4, 1, 768, 1024], P('cuts', None, 'dev'), may hold values from -6 to 6
- w_out: bfloat16 [1024, 1024], P('dev'), may hold values from -0.1875 to 0.1875
- norm_gain: float32 [1024], replicated, may hold values from 0.1 to 1.9
- hist_blocks: int32 [4, 4], replicated, may hold values from 1 to 32, as said below
- ranker_list: int32 [4, 4], replicated, may hold values from 0 to 3, as said below
- owner_ids: int32 [4, 4, 32], replicated, may hold values from -1 to 31, as said below
- slot_ids: int32 [4, 4, 32], replicated, may hold values from -1 to 7, as said below
- block_mask: int32 [4, 4, 6, 32], replicated, may hold values 0 or 1
Outputs:
- mixed: bfloat16 [4, 1, 768, 1024], P('cuts', None, 'dev')
The draws below stay inside these ranges and needn't reach their ends.
Inputs may be any that keep to these rules, and one draw needn't show every extreme that they name: `hist_blocks`: the entries of one slice sum to 64, and one request of each slice has exactly 32 blocks. `ranker_list`: each slice's row is a permutation of its 4 requests. `owner_ids`: an entry is the cut index times 8 plus the dev index of the device that holds the block, and -1 exactly where b >= hist_blocks. Every device holds exactly 2 blocks of each slice's requests. The blocks of the 4 requests of one ranker group lie on devices of one dev index (over all cuts) at most 8 times, and some group reaches 8. `slot_ids`: -1 exactly where owner_ids is -1; the blocks of all slices use every cache row of every device exactly once.
All inputs are finite; a program needn't handle non-finite values.
Results may differ from the reference program's by a relative error of at most 0.0046.
Values may be sent and summed in bfloat16 or wider, within the bound.
A program may use at most 128 MiB of HBM per device.

```python
import jax
import jax.numpy as jnp
from jax import lax

D = 1024
H = 8
DH = 128
BLK = 128
HB = 32
RQ = 4
CAND = 192
TILE = 32
OWN = 2
HD = 1024
GROUPS = 1
REQ_CUT = 4
ROWS_G = 768
CT = 6
BLOCKS = 256
N_CUTS = 4
N_DEV = 8


def history_tables(key):
    requests = N_DEV // H * RQ
    live_total = OWN * N_CUTS * N_DEV
    cycle = N_CUTS * N_DEV
    pool_size = OWN * N_CUTS
    other_entries = requests - 1
    leftover_rows = live_total - HB - other_entries
    base_share = leftover_rows // other_entries
    extra_count = leftover_rows - base_share * other_entries
    key_cuts, key_rows = jax.random.split(key)

    def one_cut(cut_key, cut_index):
        key_spread, key_order, key_top, key_rank, key_offset, key_devs = jax.random.split(cut_key, 6)
        spread_rows = jax.random.randint(key_spread, (other_entries,), 0, base_share + 1)
        rank_order = jax.random.permutation(key_order, other_entries)
        extra_share = (rank_order < extra_count).astype(jnp.int32)
        remainder = 1 + base_share + extra_share + spread_rows - jnp.roll(spread_rows, 1)
        chosen = jax.random.randint(key_top, (), 0, requests)
        positions = jnp.arange(requests, dtype=jnp.int32)
        source = jnp.clip(positions - (positions > chosen).astype(jnp.int32), 0, other_entries - 1)
        lengths = jnp.where(positions == chosen, HB, remainder[source]).astype(jnp.int32)
        ranking = jax.random.permutation(key_rank, requests).astype(jnp.int32)
        ordered_length = lengths[ranking]
        is_live = (jnp.arange(HB, dtype=jnp.int32)[None, :] < ordered_length[:, None]).reshape(-1)
        counter = jnp.cumsum(is_live.astype(jnp.int32)) - 1
        offset = jax.random.randint(key_offset, (), 0, cycle)
        spot = (counter + offset) % live_total
        owner_flat = spot % cycle
        round_index = spot // cycle
        dev_order = jax.random.permutation(key_devs, N_DEV).astype(jnp.int32)
        owner_id = owner_flat // N_DEV * N_DEV + dev_order[owner_flat % N_DEV]
        local_row = cut_index * OWN + round_index
        return (lengths, ranking, owner_id, local_row, is_live)
    lengths, ranking, owner_rank, local_rank, live_rank = jax.vmap(one_cut)(jax.random.split(key_cuts, N_CUTS), jnp.arange(N_CUTS, dtype=jnp.int32))
    shuffles = jax.vmap(lambda owner: jax.random.permutation(jax.random.fold_in(key_rows, owner), pool_size))(jnp.arange(cycle, dtype=jnp.int32)).astype(jnp.int32)
    slot_rank = shuffles[jnp.clip(owner_rank, 0, cycle - 1), local_rank]
    owner_rank = jnp.where(live_rank, owner_rank, -1)
    slot_rank = jnp.where(live_rank, slot_rank, -1)
    inverse = jnp.argsort(ranking, axis=1)
    cut_rows = jnp.arange(N_CUTS)[:, None]
    owners = owner_rank.reshape(N_CUTS, requests, HB)[cut_rows, inverse]
    slots = slot_rank.reshape(N_CUTS, requests, HB)[cut_rows, inverse]
    return (lengths, ranking, owners.astype(jnp.int32), slots.astype(jnp.int32))


def draw_hist_blocks(key, part):
    return history_tables(key)[0]


def draw_ranker_list(key, part):
    return history_tables(key)[1]


def draw_owner_ids(key, part):
    return history_tables(key)[2]


def draw_slot_ids(key, part):
    return history_tables(key)[3]


def set_ends(result, rng, low, high):
    index_at = [jax.random.randint(jax.random.fold_in(rng, axis), (), 0, length) for axis, length in enumerate(result.shape)]
    main_axis = result.shape.index(max(result.shape))
    next_to = index_at[:main_axis] + [(index_at[main_axis] + 1) % result.shape[main_axis]] + index_at[main_axis + 1:]
    return result.at[tuple(index_at)].set(low).at[tuple(next_to)].set(high)


def steps_of(rng, extent, pieces, smallest, high):
    loudness, own = 1.0, jax.random.fold_in(rng, 6)
    for dim, parts in pieces:
        draws = jnp.exp(jax.random.uniform(jax.random.fold_in(own, dim), (parts,), jnp.float32, smallest / len(pieces), high / len(pieces)))
        loudness = loudness * jnp.repeat(draws, extent[dim] // parts).reshape([-1 if axis == dim else 1 for axis in range(len(extent))])
    return loudness


def gaussian(own_key, extent, width, limit, cuts=(), kind=jnp.bfloat16):
    result = width * jax.random.normal(own_key, extent, jnp.float32)
    if cuts:
        result = result * steps_of(own_key, extent, cuts, -0.22, 0.18)
    return jnp.clip(result, -limit, limit).astype(kind)


def setup_inputs(seed: int = 0) -> dict:
    key_of = jax.random.split(jax.random.key(seed), 12)
    kv_cache = gaussian(key_of[0], (BLOCKS, BLK, 2 * HD), 1.0, 6.0, ((0, 32),))
    queries = gaussian(key_of[1], (N_CUTS, N_DEV, ROWS_G, DH), 1.0, 6.0, ((0, 4), (1, 8)))
    gates = gaussian(key_of[2], (N_CUTS, GROUPS, ROWS_G, HD), 1.0, 6.0, ((0, 4), (2, 8)))
    tokens = gaussian(key_of[3], (N_CUTS, GROUPS, ROWS_G, D), 1.0, 6.0, ((0, 4), (2, 8)))
    w_out = gaussian(key_of[4], (HD, D), HD ** -0.5, 0.1875, ((0, 8),))
    norm_gain = jnp.clip(1.0 + 0.18 * jax.random.normal(key_of[5], (HD,), jnp.float32), 0.1, 1.9)
    hist_blocks = draw_hist_blocks(jax.random.fold_in(key_of[11], 71), 0)
    ranker_list = draw_ranker_list(jax.random.fold_in(key_of[11], 71), 0)
    owner_ids = draw_owner_ids(jax.random.fold_in(key_of[11], 71), 0)
    slot_ids = draw_slot_ids(jax.random.fold_in(key_of[11], 71), 0)
    block_mask = set_ends((jax.random.randint(key_of[10], (N_CUTS, REQ_CUT, CT, HB), 0, 4) < 3).astype(jnp.int32), jax.random.fold_in(key_of[10], 1), 0, 1)
    return dict(kv_cache=kv_cache, queries=queries, gates=gates, tokens=tokens, w_out=w_out, norm_gain=norm_gain, hist_blocks=hist_blocks, ranker_list=ranker_list, owner_ids=owner_ids, slot_ids=slot_ids, block_mask=block_mask)


EPS = 1e-05

def attend_request(query, blocks, allowed):
    key_rows = blocks[:, :, :, 0, :].astype(jnp.float32)
    value_rows = blocks[:, :, :, 1, :].astype(jnp.float32)
    scores = jnp.einsum('hce,bkhe->hcbk', query.astype(jnp.float32), key_rows) * DH ** (-0.5)
    weights = (jax.nn.silu(scores) * allowed[None, :, :, None]).astype(jnp.bfloat16)
    attended = jnp.einsum('hcbk,bkhe->che', weights.astype(jnp.float32), value_rows)
    return attended.astype(jnp.bfloat16)

def reference(kv_cache, queries, gates, tokens, w_out, norm_gain, hist_blocks, ranker_list, owner_ids, slot_ids, block_mask):
    groups = N_DEV // H
    pool_size = OWN * N_CUTS
    cache_blocks = kv_cache.reshape(-1, BLK, H, 2, DH)
    query_heads = queries.reshape(N_CUTS, H, groups, RQ, CAND, DH)

    def one_request(flat_index):
        cut_index = flat_index // (groups * RQ)
        within = flat_index % (groups * RQ)
        group_index = within // RQ
        slot_index = within % RQ
        request = ranker_list[cut_index, group_index * RQ + slot_index]
        length = hist_blocks[cut_index, request]
        rows = owner_ids[cut_index, request] * pool_size + slot_ids[cut_index, request]
        blocks = cache_blocks[jnp.maximum(rows, 0)]
        is_live = (jnp.arange(HB, dtype=jnp.int32) < length).astype(jnp.int32)
        tile_mask = block_mask[cut_index, request] * is_live[None, :]
        allowed = jnp.repeat(tile_mask, TILE, axis=0).astype(jnp.float32)
        query = query_heads[cut_index, :, group_index, slot_index]
        return attend_request(query, blocks, allowed)
    attended = lax.map(one_request, jnp.arange(N_CUTS * groups * RQ, dtype=jnp.int32))
    attended = attended.reshape(N_CUTS, groups, RQ * CAND, H * DH).astype(jnp.float32)
    row_mean = lax.optimization_barrier(jnp.mean(attended, axis=-1, keepdims=True))
    centred = attended - row_mean
    variance = lax.optimization_barrier(jnp.mean(centred * centred, axis=-1, keepdims=True))
    normed = centred * lax.rsqrt(variance + EPS) * norm_gain.astype(jnp.float32)
    gated = (normed * jax.nn.silu(gates.astype(jnp.float32))).astype(jnp.bfloat16)
    projected = jnp.dot(gated.reshape(-1, H * DH), w_out, preferred_element_type=jnp.float32)
    projected = projected.reshape(N_CUTS, groups, RQ * CAND, D)
    return (tokens.astype(jnp.float32) + projected).astype(jnp.bfloat16)
```

```python
import functools

import jax
import jax.numpy as jnp
from jax import lax
from jax.experimental import pallas as pl
from jax.experimental.pallas import tpu as pltpu
from jax.sharding import PartitionSpec as P

H = 8
DH = 128
HB = 32
RQ = 4
TILE = 32


EPS = 1e-05


def ranked(selected, count):
    sequence = jnp.cumsum(selected.astype(jnp.int32), axis=-1) - 1
    picks = jnp.arange(count, dtype=jnp.int32)
    return selected[..., None, :] & (sequence[..., None, :] == picks[:, None])


def local_general(
    kv_cache,
    queries,
    gates,
    tokens,
    w_out,
    norm_gain,
    hist_blocks,
    ranker_list,
    owner_ids,
    slot_ids,
    block_mask,
):
    cut_count = lax.axis_size("cuts")
    dev_count = lax.axis_size("dev")
    this_cut = lax.axis_index("cuts")
    this_dev = lax.axis_index("dev")
    groups = dev_count // H
    group_index = this_dev % groups
    pool_size, block_items, width = kv_cache.shape
    slab_width = width // H
    head_size = slab_width // 2
    owned = pool_size // cut_count
    per_group = RQ * HB
    live_cut = owned * cut_count * dev_count
    capacity = (min(per_group, live_cut) + dev_count - 1) // dev_count
    request_count = ranker_list.shape[1]
    keys_cut = request_count * HB
    cut_rows = jnp.arange(cut_count)[:, None]
    owners_ranked = owner_ids[cut_rows, ranker_list].reshape(cut_count, keys_cut)
    slots_ranked = slot_ids[cut_rows, ranker_list].reshape(cut_count, keys_cut)
    owner_self = this_cut * dev_count + this_dev
    chosen = ranked(owners_ranked == owner_self, owned)
    send_rows = jnp.sum(jnp.where(chosen, slots_ranked[:, None, :], 0), axis=-1)
    packed = kv_cache[send_rows.reshape(-1)].reshape(cut_count, owned, block_items, width)
    arrived = lax.all_to_all(packed, "cuts", split_axis=0, concat_axis=0, tiled=True)
    owner_table = lax.dynamic_index_in_dim(owners_ranked, this_cut, 0, keepdims=False)
    sources = jnp.arange(cut_count, dtype=jnp.int32) * dev_count + this_dev
    relay_pick = ranked(owner_table[None, :] == sources[:, None], owned)
    key_index = jnp.arange(keys_cut, dtype=jnp.int32)
    key_of = jnp.sum(jnp.where(relay_pick, key_index, 0), axis=-1).reshape(pool_size)
    group_of = key_of // per_group
    sequence = jnp.arange(pool_size)
    earlier = (group_of[None, :] == group_of[:, None]) & (sequence[None, :] < sequence[:, None])
    target = group_of * capacity + jnp.sum(earlier, axis=1)
    heads_first = arrived.reshape(pool_size, block_items, H, slab_width).transpose(2, 0, 1, 3)
    outgoing = jnp.zeros((H, groups * capacity, block_items, slab_width), arrived.dtype)
    outgoing = (
        outgoing.at[:, target]
        .set(heads_first)
        .reshape(dev_count, capacity, block_items, slab_width)
    )
    received = lax.all_to_all(outgoing, "dev", split_axis=0, concat_axis=0, tiled=True)
    flat_blocks = received.reshape(dev_count * capacity, block_items, slab_width)
    cut_list = lax.dynamic_index_in_dim(ranker_list, this_cut, 0, keepdims=False)
    requests = lax.dynamic_slice_in_dim(cut_list, group_index * RQ, RQ)
    lengths = lax.dynamic_index_in_dim(hist_blocks, this_cut, 0, keepdims=False)[requests]
    group_mask = lax.dynamic_index_in_dim(block_mask, this_cut, 0, keepdims=False)[requests]
    live_blocks = jnp.arange(HB, dtype=jnp.int32)[None, :] < lengths[:, None]
    is_live = live_blocks.reshape(per_group)
    group_owners = lax.dynamic_slice_in_dim(owner_table, group_index * per_group, per_group)
    src_dev = group_owners % dev_count
    src_cut = group_owners // dev_count
    position = jnp.arange(per_group)
    before = (
        is_live[None, :]
        & (src_dev[None, :] == src_dev[:, None])
        & (
            (src_cut[None, :] < src_cut[:, None])
            | (src_cut[None, :] == src_cut[:, None]) & (position[None, :] < position[:, None])
        )
    )
    slot_of = jnp.where(is_live, src_dev * capacity + jnp.sum(before, axis=1), 0).reshape(RQ, HB)
    tile_mask = (group_mask * live_blocks[:, None, :].astype(jnp.int32)).astype(jnp.float32)
    query_all = queries.reshape(RQ, -1, head_size)

    def attend(query, slot_rows, tiles):
        blocks = flat_blocks[slot_rows]
        key_rows = blocks[:, :, :head_size].reshape(-1, head_size)
        value_rows = blocks[:, :, head_size:].reshape(-1, head_size)
        scores = jnp.einsum(
            "ce,ke->ck", query, key_rows, preferred_element_type=jnp.float32
        ) * DH ** (-0.5)
        allowed = jnp.repeat(tiles, TILE, axis=0)
        rows_here = query.shape[0]
        weights = jax.nn.silu(scores).reshape(rows_here, HB, block_items) * allowed[:, :, None]
        weights = weights.reshape(rows_here, -1).astype(jnp.bfloat16)
        return jnp.dot(weights, value_rows, preferred_element_type=jnp.float32).astype(jnp.bfloat16)

    attended = lax.map(
        lambda parts: attend(parts[0], parts[1], parts[2]), (query_all, slot_of, tile_mask)
    )
    rows_each = attended.shape[0] * attended.shape[1] // dev_count
    back = lax.all_to_all(
        attended.reshape(dev_count, rows_each, head_size),
        "dev",
        split_axis=0,
        concat_axis=0,
        tiled=True,
    )
    gathered = back.reshape(H, groups, rows_each, head_size).transpose(1, 2, 0, 3)
    gathered = gathered.reshape(groups * rows_each, H * head_size).astype(jnp.float32)
    row_mean = jnp.mean(gathered, axis=-1, keepdims=True)
    centred = gathered - row_mean
    variance = jnp.mean(centred * centred, axis=-1, keepdims=True)
    normed = centred * lax.rsqrt(variance + EPS) * norm_gain
    gate_rows = gates.reshape(-1, H * head_size).astype(jnp.float32)
    gated = (normed * jax.nn.silu(gate_rows)).astype(jnp.bfloat16)
    projected = jnp.dot(
        gated, lax.all_gather(w_out, "dev", axis=0, tiled=True), preferred_element_type=jnp.float32
    )
    return (tokens.astype(jnp.float32) + projected.reshape(tokens.shape)).astype(jnp.bfloat16)


CUTS = 4
DEVS = 8
STAGES = 4
MESH = pl.DeviceIdType.MESH


def rem(a, b):
    return lax.rem(a, jnp.int32(b))


def div(a, b):
    return lax.div(a, jnp.int32(b))


def fused_kernel(
    rows_ref,
    mask_ref,
    q_ref,
    gates_ref,
    tokens_ref,
    w_ref,
    gain_ref,
    kv_ref,
    out_ref,
    kv0,
    kv1,
    kv2,
    kv3,
    pk,
    rx,
    qbuf,
    acc,
    ab,
    parts,
    wbuf,
    load_sem,
    kv_send,
    kv_recv,
    q_send,
    q_recv,
    p_send,
    p_recv,
    w_send,
    w_recv,
):
    loaded = (kv0, kv1, kv2, kv3)
    cut = lax.axis_index("cuts")
    dev = lax.axis_index("dev")
    x, y = rem(cut, 2), div(cut, 2)
    z, core = div(dev, 2), rem(dev, 2)

    def cut_at(off):
        return rem(y + div(off, 2), 2) * 2 + rem(x + rem(off, 2), 2)

    def core_at(off):
        return rem(core + off, 2)

    def load(s, oh):
        head = rem(z + s, 4) * 2 + core_at(oh)
        columns = pl.ds(pl.multiple_of(head * 256, 256), 256)
        return pltpu.make_async_copy(
            kv_ref.at[:, :, columns], loaded[s].at[oh], load_sem.at[s, oh]
        )

    for s in range(STAGES):
        for oh in range(2):
            load(s, oh).start()

    barrier = pltpu.get_barrier_semaphore()
    for o in range(2, 8):
        pl.semaphore_signal(
            barrier,
            inc=1,
            device_id=(cut_at(o // 2), z * 2 + core_at(o % 2)),
            device_id_type=MESH,
        )
    for o in range(1, 8):
        pl.semaphore_signal(
            barrier,
            inc=1,
            device_id=(cut, rem(z + o // 2, 4) * 2 + core_at(o % 2)),
            device_id_type=MESH,
        )
    pl.semaphore_wait(barrier, 13)

    def kv_copy(s, o):
        return pltpu.make_async_remote_copy(
            src_ref=pk.at[s, o],
            dst_ref=rx.at[s, o],
            send_sem=kv_send.at[s, o],
            recv_sem=kv_recv.at[s, o],
            device_id=(cut_at(div(o, 2)), z * 2 + core_at(rem(o, 2))),
            device_id_type=MESH,
        )

    def q_copy(o):
        return pltpu.make_async_remote_copy(
            src_ref=q_ref,
            dst_ref=qbuf.at[4 - o],
            send_sem=q_send.at[4 - o],
            recv_sem=q_recv.at[4 - o],
            device_id=(cut, rem(z + o, 4) * 2 + core),
            device_id_type=MESH,
        )

    def p_copy(s, o):
        where = rem(z + div(o, 2), 4) * 2 + core_at(rem(o, 2))
        return pltpu.make_async_remote_copy(
            src_ref=ab.at[s, where],
            dst_ref=parts.at[s, o],
            send_sem=p_send.at[s, o],
            recv_sem=p_recv.at[s, o],
            device_id=(cut, where),
            device_id_type=MESH,
        )

    def w_copy(o):
        if o % 2:
            source = w_ref if o == 1 else wbuf.at[o - 1]
            where = z * 2 + core_at(1)
        else:
            source = w_ref
            where = rem(z + o // 2, 4) * 2 + core
        return pltpu.make_async_remote_copy(
            src_ref=source,
            dst_ref=wbuf.at[o],
            send_sem=w_send.at[o],
            recv_sem=w_recv.at[o],
            device_id=(cut, where),
            device_id_type=MESH,
        )

    def pack(s):
        for oh in range(2):
            load(s, oh).wait()

        def one(i, carry):
            oc = 3 - i
            for j in range(2):
                slot = rows_ref[cut_at(oc), j]
                for oh in range(2):
                    pk[s, oc * 2 + oh, j] = loaded[s][oh, slot]
            for oh in range(2):

                @pl.when(oc * 2 + oh > 0)
                def _():
                    kv_copy(s, oc * 2 + oh).start()

            return carry

        lax.fori_loop(jnp.int32(0), jnp.int32(4), one, 0)
        rx[s, 0] = pk[s, 0]

    pack(0)
    for o in (3, 2, 1):
        q_copy(o).start()
    pack(1)
    for o in (6, 4, 2, 1):
        w_copy(o).start()
    qbuf[0] = q_ref[...]

    def stage(s, carry):
        @pl.when(s > 0)
        def _():
            q_copy(4 - s).wait_recv()

        acc[...] = jnp.zeros_like(acc)

        def block(o, inner):
            @pl.when(o > 0)
            def _():
                kv_copy(s, o).wait_recv()

            keys = rx[s, o, :, :, 0:128].reshape(256, 128)
            values = rx[s, o, :, :, 128:256].reshape(256, 128)
            for k in range(RQ):
                rows = pl.ds(k * 192, 192)
                scores = lax.dot_general(
                    qbuf[s, rows, :],
                    keys,
                    (((1,), (1,)), ((), ())),
                    preferred_element_type=jnp.float32,
                )
                half = scores.reshape(6, TILE, 256) * mask_ref[o, k][:6, None, :]
                weights = (half + half * jnp.tanh(half)).reshape(192, 256)
                acc[rows, :] += jnp.dot(
                    weights.astype(jnp.bfloat16), values, preferred_element_type=jnp.float32
                )
            return inner

        lax.fori_loop(jnp.int32(0), jnp.int32(8), block, 0)
        ab[s] = acc[...].reshape(8, 96, 128).astype(jnp.bfloat16)

        def send(o, inner):
            p_copy(s, o).start()
            return inner

        lax.fori_loop(jnp.int32(1), jnp.int32(8), send, 0)
        parts[s, 0] = ab[s, z * 2 + core]

        @pl.when(s == 0)
        def _():
            pack(2)

        @pl.when(s == 1)
        def _():
            pack(3)

        @pl.when(s == 2)
        def _():
            for o in (2, 4, 6):
                w_copy(o).wait_recv()
                w_copy(o + 1).start()

        return carry

    lax.fori_loop(jnp.int32(0), jnp.int32(STAGES), stage, 0)

    gate_list, total_list = [], []
    for pr in range(4):
        for oh in range(2):
            head = rem(z + pr, 4) * 2 + core_at(oh)
            columns = pl.ds(pl.multiple_of(head * 128, 128), 128)
            gate = gates_ref[:, columns].astype(jnp.float32)
            gate_list.append(gate / (1.0 + jnp.exp(-gate)) * gain_ref[:, columns])
    for o in (1, 3, 5, 7):
        w_copy(o).wait_recv()
    for s in range(STAGES):
        for o in range(1, 8):
            p_copy(jnp.int32(s), jnp.int32(o)).wait_recv()
    for pr in range(4):
        for oh in range(2):
            total = parts[pr, oh].astype(jnp.float32)
            for ok in range(1, 4):
                total += parts[(pr + ok) % 4, ok * 2 + oh].astype(jnp.float32)
            total_list.append(total)
    features = float(H * DH)
    mean = jnp.sum(sum(total_list), axis=-1, keepdims=True) / features
    centred = [total - mean for total in total_list]
    squares = sum(part * part for part in centred)
    variance = jnp.sum(squares, axis=-1, keepdims=True) / features
    scale = lax.rsqrt(variance + EPS)
    projected = tokens_ref[...].astype(jnp.float32)
    for pr in range(4):
        ow = (4 - pr) % 4
        for oh in range(2):
            r = pr * 2 + oh
            gated = (centred[r] * scale * gate_list[r]).astype(jnp.bfloat16)
            weight = w_ref[...] if ow * 2 + oh == 0 else wbuf[ow * 2 + oh]
            projected += jnp.dot(gated, weight, preferred_element_type=jnp.float32)
    out_ref[...] = projected.astype(out_ref.dtype)

    for o in (1, 2, 3):
        q_copy(o).wait_send()
    for o in range(1, 8):
        w_copy(o).wait_send()

    def drain(i, carry):
        s, o = div(i, 7), rem(i, 7) + 1
        kv_copy(s, o).wait_send()
        p_copy(s, o).wait_send()
        return carry

    lax.fori_loop(jnp.int32(0), jnp.int32(28), drain, 0)


def local_fused(
    kv_cache,
    queries,
    gates,
    tokens,
    w_out,
    norm_gain,
    hist_blocks,
    ranker_list,
    owner_ids,
    slot_ids,
    block_mask,
):
    cut = lax.axis_index("cuts")
    dev = lax.axis_index("dev")
    me = cut * DEVS + dev
    position = jnp.arange(RQ * HB, dtype=jnp.int32)
    coded = position * DEVS + slot_ids.reshape(CUTS, RQ * HB)
    mine = owner_ids.reshape(CUTS, RQ * HB) == me
    first = jnp.min(jnp.where(mine, coded, 1 << 20), axis=-1)
    last = jnp.max(jnp.where(mine, coded, 0), axis=-1)
    send_rows = jnp.stack([first, last], axis=-1) % DEVS

    offset = jnp.arange(8, dtype=jnp.int32)
    sources = (cut ^ (offset // 2)) * DEVS + (dev ^ (offset % 2))
    owners = lax.dynamic_index_in_dim(owner_ids, cut, 0, keepdims=False).reshape(-1)
    theirs = owners[None, :] == sources[:, None]
    lowest = jnp.min(jnp.where(theirs, position, 1 << 20), axis=-1)
    highest = jnp.max(jnp.where(theirs, position, -1), axis=-1)
    places = jnp.stack([lowest, highest], axis=-1)
    live = jnp.arange(HB, dtype=jnp.int32) < lax.dynamic_index_in_dim(
        hist_blocks, cut, 0, keepdims=False
    )[:, None]
    visible = lax.dynamic_index_in_dim(block_mask, cut, 0, keepdims=False) * live[:, None, :]
    ranks = lax.dynamic_index_in_dim(ranker_list, cut, 0, keepdims=False)
    is_ranked = ranks[:, None] == jnp.arange(RQ, dtype=jnp.int32)
    table = jnp.where(is_ranked[:, None, :, None], visible.transpose(1, 0, 2)[None], 0)
    table = table.reshape(RQ, -1, RQ * HB).astype(jnp.bfloat16)
    table = jnp.pad(table, ((0, 0), (0, 8 - table.shape[1]), (0, 0))).reshape(RQ * 8, RQ * HB)
    spread = jnp.repeat(places, 128, axis=-1)
    onehot = (position[None, :, None] == spread[:, None, :]).astype(jnp.bfloat16)
    allowed = jnp.einsum(
        "otp,opn->otn",
        jnp.broadcast_to(table[None], (8,) + table.shape),
        onehot,
        preferred_element_type=jnp.float32,
    ) * (0.5 * DH ** (-0.5))
    allowed = allowed.reshape(8, RQ, 8, 256)

    rows = gates.shape[2]
    vmem = pl.BlockSpec(memory_space=pltpu.VMEM)
    bf16 = jnp.bfloat16
    mixed = pl.pallas_call(
        fused_kernel,
        out_shape=jax.ShapeDtypeStruct((rows, H * DH), bf16),
        in_specs=[pl.BlockSpec(memory_space=pltpu.SMEM)]
        + [vmem] * 6
        + [pl.BlockSpec(memory_space=pl.ANY)],
        out_specs=vmem,
        scratch_shapes=[
            pltpu.VMEM((2, 8, 128, 256), bf16),
            pltpu.VMEM((2, 8, 128, 256), bf16),
            pltpu.VMEM((2, 8, 128, 256), bf16),
            pltpu.VMEM((2, 8, 128, 256), bf16),
            pltpu.VMEM((STAGES, 8, 2, 128, 256), bf16),
            pltpu.VMEM((STAGES, 8, 2, 128, 256), bf16),
            pltpu.VMEM((STAGES, 768, 128), bf16),
            pltpu.VMEM((768, 128), jnp.float32),
            pltpu.VMEM((STAGES, 8, 96, 128), bf16),
            pltpu.VMEM((STAGES, 8, 96, 128), bf16),
            pltpu.VMEM((8, 128, 1024), bf16),
            pltpu.SemaphoreType.DMA((STAGES, 2)),
            pltpu.SemaphoreType.DMA((STAGES, 8)),
            pltpu.SemaphoreType.DMA((STAGES, 8)),
            pltpu.SemaphoreType.DMA((4,)),
            pltpu.SemaphoreType.DMA((4,)),
            pltpu.SemaphoreType.DMA((STAGES, 8)),
            pltpu.SemaphoreType.DMA((STAGES, 8)),
            pltpu.SemaphoreType.DMA((8,)),
            pltpu.SemaphoreType.DMA((8,)),
        ],
        compiler_params=pltpu.CompilerParams(
            collective_id=0, has_side_effects=True, vmem_limit_bytes=40 * 1024 * 1024
        ),
        cost_estimate=pl.CostEstimate(
            flops=4 * 4 * 768 * 2048 * 128, bytes_accessed=8 << 20, transcendentals=4 * 768 * 2048
        ),
    )(
        send_rows,
        allowed,
        queries.reshape(queries.shape[2:]),
        gates.reshape(rows, H * DH),
        tokens.reshape(rows, H * DH),
        w_out,
        norm_gain.reshape(1, H * DH),
        kv_cache,
    )
    return mixed.reshape(tokens.shape)


def solution(mesh):
    fused = mesh.shape["cuts"] == CUTS and mesh.shape["dev"] == DEVS
    local = local_fused if fused else local_general
    return jax.shard_map(
        local,
        mesh=mesh,
        in_specs=(
            P(("cuts", "dev"), None, None),
            P("cuts", "dev", None, None),
            P("cuts", None, "dev", None),
            P("cuts", None, "dev", None),
            P("dev", None),
            P(),
            P(),
            P(),
            P(),
            P(),
            P(),
        ),
        out_specs=P("cuts", None, "dev", None),
        check_vma=False,
    )
```

```python
import functools

import jax
import jax.numpy as jnp
from jax import lax
from jax.experimental import pallas as pl
from jax.experimental.pallas import tpu as pltpu
from jax.sharding import PartitionSpec as P

H = 8
DH = 128
HB = 32
RQ = 4
TILE = 32


EPS = 1e-05


def ranked(selected, count):
    sequence = jnp.cumsum(selected.astype(jnp.int32), axis=-1) - 1
    picks = jnp.arange(count, dtype=jnp.int32)
    return selected[..., None, :] & (sequence[..., None, :] == picks[:, None])


def local_general(
    kv_cache,
    queries,
    gates,
    tokens,
    w_out,
    norm_gain,
    hist_blocks,
    ranker_list,
    owner_ids,
    slot_ids,
    block_mask,
):
    cut_count = lax.axis_size("cuts")
    dev_count = lax.axis_size("dev")
    this_cut = lax.axis_index("cuts")
    this_dev = lax.axis_index("dev")
    groups = dev_count // H
    group_index = this_dev % groups
    pool_size, block_items, width = kv_cache.shape
    slab_width = width // H
    head_size = slab_width // 2
    owned = pool_size // cut_count
    per_group = RQ * HB
    live_cut = owned * cut_count * dev_count
    capacity = (min(per_group, live_cut) + dev_count - 1) // dev_count
    request_count = ranker_list.shape[1]
    keys_cut = request_count * HB
    cut_rows = jnp.arange(cut_count)[:, None]
    owners_ranked = owner_ids[cut_rows, ranker_list].reshape(cut_count, keys_cut)
    slots_ranked = slot_ids[cut_rows, ranker_list].reshape(cut_count, keys_cut)
    owner_self = this_cut * dev_count + this_dev
    chosen = ranked(owners_ranked == owner_self, owned)
    send_rows = jnp.sum(jnp.where(chosen, slots_ranked[:, None, :], 0), axis=-1)
    packed = kv_cache[send_rows.reshape(-1)].reshape(cut_count, owned, block_items, width)
    arrived = lax.all_to_all(packed, "cuts", split_axis=0, concat_axis=0, tiled=True)
    owner_table = lax.dynamic_index_in_dim(owners_ranked, this_cut, 0, keepdims=False)
    sources = jnp.arange(cut_count, dtype=jnp.int32) * dev_count + this_dev
    relay_pick = ranked(owner_table[None, :] == sources[:, None], owned)
    key_index = jnp.arange(keys_cut, dtype=jnp.int32)
    key_of = jnp.sum(jnp.where(relay_pick, key_index, 0), axis=-1).reshape(pool_size)
    group_of = key_of // per_group
    sequence = jnp.arange(pool_size)
    earlier = (group_of[None, :] == group_of[:, None]) & (sequence[None, :] < sequence[:, None])
    target = group_of * capacity + jnp.sum(earlier, axis=1)
    heads_first = arrived.reshape(pool_size, block_items, H, slab_width).transpose(2, 0, 1, 3)
    outgoing = jnp.zeros((H, groups * capacity, block_items, slab_width), arrived.dtype)
    outgoing = (
        outgoing.at[:, target]
        .set(heads_first)
        .reshape(dev_count, capacity, block_items, slab_width)
    )
    received = lax.all_to_all(outgoing, "dev", split_axis=0, concat_axis=0, tiled=True)
    flat_blocks = received.reshape(dev_count * capacity, block_items, slab_width)
    cut_list = lax.dynamic_index_in_dim(ranker_list, this_cut, 0, keepdims=False)
    requests = lax.dynamic_slice_in_dim(cut_list, group_index * RQ, RQ)
    lengths = lax.dynamic_index_in_dim(hist_blocks, this_cut, 0, keepdims=False)[requests]
    group_mask = lax.dynamic_index_in_dim(block_mask, this_cut, 0, keepdims=False)[requests]
    live_blocks = jnp.arange(HB, dtype=jnp.int32)[None, :] < lengths[:, None]
    is_live = live_blocks.reshape(per_group)
    group_owners = lax.dynamic_slice_in_dim(owner_table, group_index * per_group, per_group)
    src_dev = group_owners % dev_count
    src_cut = group_owners // dev_count
    position = jnp.arange(per_group)
    before = (
        is_live[None, :]
        & (src_dev[None, :] == src_dev[:, None])
        & (
            (src_cut[None, :] < src_cut[:, None])
            | (src_cut[None, :] == src_cut[:, None]) & (position[None, :] < position[:, None])
        )
    )
    slot_of = jnp.where(is_live, src_dev * capacity + jnp.sum(before, axis=1), 0).reshape(RQ, HB)
    tile_mask = (group_mask * live_blocks[:, None, :].astype(jnp.int32)).astype(jnp.float32)
    query_all = queries.reshape(RQ, -1, head_size)

    def attend(query, slot_rows, tiles):
        blocks = flat_blocks[slot_rows]
        key_rows = blocks[:, :, :head_size].reshape(-1, head_size)
        value_rows = blocks[:, :, head_size:].reshape(-1, head_size)
        scores = jnp.einsum(
            "ce,ke->ck", query, key_rows, preferred_element_type=jnp.float32
        ) * DH ** (-0.5)
        allowed = jnp.repeat(tiles, TILE, axis=0)
        rows_here = query.shape[0]
        weights = jax.nn.silu(scores).reshape(rows_here, HB, block_items) * allowed[:, :, None]
        weights = weights.reshape(rows_here, -1).astype(jnp.bfloat16)
        return jnp.dot(weights, value_rows, preferred_element_type=jnp.float32).astype(jnp.bfloat16)

    attended = lax.map(
        lambda parts: attend(parts[0], parts[1], parts[2]), (query_all, slot_of, tile_mask)
    )
    rows_each = attended.shape[0] * attended.shape[1] // dev_count
    back = lax.all_to_all(
        attended.reshape(dev_count, rows_each, head_size),
        "dev",
        split_axis=0,
        concat_axis=0,
        tiled=True,
    )
    gathered = back.reshape(H, groups, rows_each, head_size).transpose(1, 2, 0, 3)
    gathered = gathered.reshape(groups * rows_each, H * head_size).astype(jnp.float32)
    row_mean = jnp.mean(gathered, axis=-1, keepdims=True)
    centred = gathered - row_mean
    variance = jnp.mean(centred * centred, axis=-1, keepdims=True)
    normed = centred * lax.rsqrt(variance + EPS) * norm_gain
    gate_rows = gates.reshape(-1, H * head_size).astype(jnp.float32)
    gated = (normed * jax.nn.silu(gate_rows)).astype(jnp.bfloat16)
    projected = jnp.dot(
        gated, lax.all_gather(w_out, "dev", axis=0, tiled=True), preferred_element_type=jnp.float32
    )
    return (tokens.astype(jnp.float32) + projected.reshape(tokens.shape)).astype(jnp.bfloat16)


CUTS = 4
DEVS = 8
STAGES = 4
MESH = pl.DeviceIdType.MESH


def rem(a, b):
    return lax.rem(a, jnp.int32(b))


def div(a, b):
    return lax.div(a, jnp.int32(b))


def fused_kernel(
    hist_ref,
    rank_ref,
    owner_hbm,
    slot_hbm,
    seen_hbm,
    q_hbm,
    gates_hbm,
    tokens_hbm,
    w_hbm,
    gain_hbm,
    kv_hbm,
    out_ref,
    owner_ref,
    slot_ref,
    seen_ref,
    gates_ref,
    tokens_ref,
    gain_ref,
    rows_ref,
    place_ref,
    mask_ref,
    kv0,
    kv1,
    kv2,
    kv3,
    pk,
    rx,
    qbuf,
    acc,
    ab,
    parts,
    wbuf,
    load_sem,
    kv_send,
    kv_recv,
    q_send,
    q_recv,
    p_send,
    p_recv,
    w_send,
    w_recv,
    table_sem,
):
    loaded = (kv0, kv1, kv2, kv3)
    cut = lax.axis_index("cuts")
    dev = lax.axis_index("dev")
    x, y = rem(cut, 2), div(cut, 2)
    z, core = div(dev, 2), rem(dev, 2)

    def cut_at(off):
        return rem(y + div(off, 2), 2) * 2 + rem(x + rem(off, 2), 2)

    def core_at(off):
        return rem(core + off, 2)

    def load(s, oh):
        head = rem(z + s, 4) * 2 + core_at(oh)
        columns = pl.ds(pl.multiple_of(head * 256, 256), 256)
        return pltpu.make_async_copy(
            kv_hbm.at[:, :, columns], loaded[s].at[oh], load_sem.at[s, oh]
        )

    fetch = [
        pltpu.make_async_copy(source, target, table_sem.at[i])
        for i, (source, target) in enumerate(
            (
                (owner_hbm, owner_ref),
                (slot_hbm, slot_ref),
                (seen_hbm, seen_ref),
                (q_hbm, qbuf.at[0]),
                (w_hbm, wbuf.at[z, 0]),
                (gates_hbm, gates_ref),
                (tokens_hbm, tokens_ref),
                (gain_hbm, gain_ref),
            )
        )
    ]
    for i in (0, 1):
        fetch[i].start()
    for oh in range(2):
        load(0, oh).start()
    for i in (3, 2, 4):
        fetch[i].start()
    for s in range(1, STAGES):
        for oh in range(2):
            load(s, oh).start()
    for i in (5, 6, 7):
        fetch[i].start()

    barrier = pltpu.get_barrier_semaphore()
    for o in range(2, 8):
        pl.semaphore_signal(
            barrier,
            inc=1,
            device_id=(cut_at(o // 2), z * 2 + core_at(o % 2)),
            device_id_type=MESH,
        )
    for o in range(1, 8):
        pl.semaphore_signal(
            barrier,
            inc=1,
            device_id=(cut, rem(z + o // 2, 4) * 2 + core_at(o % 2)),
            device_id_type=MESH,
        )
    position = lax.broadcasted_iota(jnp.int32, (RQ, HB), 0) * HB + lax.broadcasted_iota(
        jnp.int32, (RQ, HB), 1
    )
    for i in (0, 1):
        fetch[i].wait()
    for oc in range(CUTS):
        mine = owner_ref[cut_at(oc)] == cut * DEVS + dev
        coded = position * DEVS + slot_ref[cut_at(oc)]
        rows_ref[oc * 2] = rem(jnp.min(jnp.where(mine, coded, 1 << 20)), DEVS)
        rows_ref[oc * 2 + 1] = rem(jnp.max(jnp.where(mine, coded, 0)), DEVS)
    pl.semaphore_wait(barrier, 13)

    def kv_copy(s, o):
        return pltpu.make_async_remote_copy(
            src_ref=pk.at[s, o],
            dst_ref=rx.at[s, o],
            send_sem=kv_send.at[s, o],
            recv_sem=kv_recv.at[s, o],
            device_id=(cut_at(div(o, 2)), z * 2 + core_at(rem(o, 2))),
            device_id_type=MESH,
        )

    def q_copy(o):
        return pltpu.make_async_remote_copy(
            src_ref=qbuf.at[0],
            dst_ref=qbuf.at[4 - o],
            send_sem=q_send.at[4 - o],
            recv_sem=q_recv.at[4 - o],
            device_id=(cut, rem(z + o, 4) * 2 + core),
            device_id_type=MESH,
        )

    def p_copy(s, o):
        where = rem(z + div(o, 2), 4) * 2 + core_at(rem(o, 2))
        return pltpu.make_async_remote_copy(
            src_ref=ab.at[s, where],
            dst_ref=parts.at[s, o],
            send_sem=p_send.at[s, o],
            recv_sem=p_recv.at[s, o],
            device_id=(cut, where),
            device_id_type=MESH,
        )

    def w_copy(zs, way):
        where = (rem(z + 1, 4) * 2 + core, rem(z + 3, 4) * 2 + core, z * 2 + core_at(1))[way]
        return pltpu.make_async_remote_copy(
            src_ref=wbuf.at[zs, 0],
            dst_ref=wbuf.at[zs, way // 2],
            send_sem=w_send.at[zs, way],
            recv_sem=w_recv.at[zs, way // 2],
            device_id=(cut, where),
            device_id_type=MESH,
        )

    def w_each(d, use):
        for way, zs in ((0, z - d), (1, z + d)):

            @pl.when((zs >= 0) & (zs < 4))
            def _():
                @pl.when((z < 3) if way == 0 else (z > 0))
                def _():
                    use(zs, way)

                if d > 0 or way == 0:
                    use(zs, 2)

    def w_step(d):
        for way, zs in ((0, z - d), (1, z + d)):

            @pl.when((zs >= 0) & (zs < 4))
            def _():
                w_copy(zs, way).wait_recv()

        w_each(d, lambda zs, way: w_copy(zs, way).start())

    def pack(s):
        for oh in range(2):
            load(s, oh).wait()

        def one(i, carry):
            oc = 3 - i
            for j in range(2):
                slot = rows_ref[oc * 2 + j]
                for oh in range(2):
                    pk[s, oc * 2 + oh, j] = loaded[s][oh, slot]
            for oh in range(2):

                @pl.when(oc * 2 + oh > 0)
                def _():
                    kv_copy(s, oc * 2 + oh).start()

            return carry

        lax.fori_loop(jnp.int32(0), jnp.int32(4), one, 0)
        rx[s, 0] = pk[s, 0]

    pack(0)
    fetch[3].wait()
    for o in (3, 2, 1):
        q_copy(o).start()
    pack(1)
    fetch[4].wait()
    w_each(0, lambda zs, way: w_copy(zs, way).start())

    owners = owner_ref[cut]
    for o in range(8):
        theirs = owners == cut_at(o // 2) * DEVS + z * 2 + core_at(o % 2)
        lowest = jnp.min(jnp.where(theirs, position, 1 << 20))
        highest = jnp.max(jnp.where(theirs, position, -1))
        place_ref[:, o * 256 : o * 256 + 128] = jnp.full((1, 128), lowest, jnp.int32)
        place_ref[:, o * 256 + 128 : o * 256 + 256] = jnp.full((1, 128), highest, jnp.int32)
    fetch[2].wait()
    for k in range(RQ):
        request = rank_ref[cut, k]
        seen = seen_ref[cut, request]
        live = lax.broadcasted_iota(jnp.int32, seen.shape, 1) < hist_ref[cut, request]
        seen = jnp.where(live, seen, 0).astype(jnp.float32).astype(jnp.bfloat16)
        index = lax.broadcasted_iota(jnp.int32, (HB, 2048), 0) + request * HB
        onehot = jnp.where(index == place_ref[...], 1.0, 0.0).astype(jnp.bfloat16)
        allowed = jnp.dot(seen, onehot, preferred_element_type=jnp.float32)
        mask_ref[k, 0:6, :] = allowed * (0.5 * DH ** (-0.5))

    def stage(s, carry):
        @pl.when(s > 0)
        def _():
            q_copy(4 - s).wait_recv()

        acc[...] = jnp.zeros_like(acc)

        def block(o, inner):
            @pl.when(o > 0)
            def _():
                kv_copy(s, o).wait_recv()

            keys = rx[s, o, :, :, 0:128].reshape(256, 128)
            values = rx[s, o, :, :, 128:256].reshape(256, 128)
            for k in range(RQ):
                rows = pl.ds(k * 192, 192)
                scores = lax.dot_general(
                    qbuf[s, rows, :],
                    keys,
                    (((1,), (1,)), ((), ())),
                    preferred_element_type=jnp.float32,
                )
                allowed = mask_ref[k, 0:6, pl.ds(pl.multiple_of(o * 256, 256), 256)]
                half = scores.reshape(6, TILE, 256) * allowed[:, None, :]
                weights = (half + half * jnp.tanh(half)).reshape(192, 256)
                acc[rows, :] += jnp.dot(
                    weights.astype(jnp.bfloat16), values, preferred_element_type=jnp.float32
                )
            return inner

        lax.fori_loop(jnp.int32(0), jnp.int32(8), block, 0)
        ab[s] = acc[...].reshape(8, 96, 128).astype(jnp.bfloat16)

        def send(o, inner):
            p_copy(s, o).start()
            return inner

        lax.fori_loop(jnp.int32(1), jnp.int32(8), send, 0)
        parts[s, 0] = ab[s, z * 2 + core]

        @pl.when(s == 0)
        def _():
            pack(2)
            w_step(1)

        @pl.when(s == 1)
        def _():
            pack(3)
            w_step(2)

        @pl.when(s == 2)
        def _():
            w_step(3)

        return carry

    lax.fori_loop(jnp.int32(0), jnp.int32(STAGES), stage, 0)

    gate_list, total_list = [], []
    for i in (5, 6, 7):
        fetch[i].wait()
    for pr in range(4):
        for oh in range(2):
            head = rem(z + pr, 4) * 2 + core_at(oh)
            columns = pl.ds(pl.multiple_of(head * 128, 128), 128)
            gate = gates_ref[:, columns].astype(jnp.float32)
            gate_list.append(gate / (1.0 + jnp.exp(-gate)) * gain_ref[:, columns])
    for zs in range(4):
        w_copy(zs, 2).wait_recv()
    for s in range(STAGES):
        for o in range(1, 8):
            p_copy(jnp.int32(s), jnp.int32(o)).wait_recv()
    for pr in range(4):
        for oh in range(2):
            total = parts[pr, oh].astype(jnp.float32)
            for ok in range(1, 4):
                total += parts[(pr + ok) % 4, ok * 2 + oh].astype(jnp.float32)
            total_list.append(total)
    features = float(H * DH)
    mean = jnp.sum(sum(total_list), axis=-1, keepdims=True) / features
    centred = [total - mean for total in total_list]
    squares = sum(part * part for part in centred)
    variance = jnp.sum(squares, axis=-1, keepdims=True) / features
    scale = lax.rsqrt(variance + EPS)
    projected = tokens_ref[...].astype(jnp.float32)
    for pr in range(4):
        zs = rem(z + pr, 4)
        for oh in range(2):
            r = pr * 2 + oh
            gated = (centred[r] * scale * gate_list[r]).astype(jnp.bfloat16)
            projected += jnp.dot(gated, wbuf[zs, oh], preferred_element_type=jnp.float32)
    out_ref[...] = projected.astype(out_ref.dtype)

    for o in (1, 2, 3):
        q_copy(o).wait_send()
    for d in range(4):
        w_each(d, lambda zs, way: w_copy(zs, way).wait_send())

    def drain(i, carry):
        s, o = div(i, 7), rem(i, 7) + 1
        kv_copy(s, o).wait_send()
        p_copy(s, o).wait_send()
        return carry

    lax.fori_loop(jnp.int32(0), jnp.int32(28), drain, 0)


def local_fused(
    kv_cache,
    queries,
    gates,
    tokens,
    w_out,
    norm_gain,
    hist_blocks,
    ranker_list,
    owner_ids,
    slot_ids,
    block_mask,
):
    rows = gates.shape[2]
    vmem = pl.BlockSpec(memory_space=pltpu.VMEM)
    bf16 = jnp.bfloat16
    mixed = pl.pallas_call(
        fused_kernel,
        out_shape=jax.ShapeDtypeStruct((rows, H * DH), bf16),
        in_specs=[pl.BlockSpec(memory_space=pltpu.SMEM)] * 2
        + [pl.BlockSpec(memory_space=pl.ANY)] * 9,
        out_specs=vmem,
        scratch_shapes=[
            pltpu.VMEM(owner_ids.shape, jnp.int32),
            pltpu.VMEM(slot_ids.shape, jnp.int32),
            pltpu.VMEM(block_mask.shape, jnp.int32),
            pltpu.VMEM((rows, H * DH), bf16),
            pltpu.VMEM((rows, H * DH), bf16),
            pltpu.VMEM((1, H * DH), jnp.float32),
            pltpu.SMEM((8,), jnp.int32),
            pltpu.VMEM((1, 2048), jnp.int32),
            pltpu.VMEM((RQ, 8, 2048), jnp.float32),
            pltpu.VMEM((2, 8, 128, 256), bf16),
            pltpu.VMEM((2, 8, 128, 256), bf16),
            pltpu.VMEM((2, 8, 128, 256), bf16),
            pltpu.VMEM((2, 8, 128, 256), bf16),
            pltpu.VMEM((STAGES, 8, 2, 128, 256), bf16),
            pltpu.VMEM((STAGES, 8, 2, 128, 256), bf16),
            pltpu.VMEM((STAGES, 768, 128), bf16),
            pltpu.VMEM((768, 128), jnp.float32),
            pltpu.VMEM((STAGES, 8, 96, 128), bf16),
            pltpu.VMEM((STAGES, 8, 96, 128), bf16),
            pltpu.VMEM((4, 2, 128, 1024), bf16),
            pltpu.SemaphoreType.DMA((STAGES, 2)),
            pltpu.SemaphoreType.DMA((STAGES, 8)),
            pltpu.SemaphoreType.DMA((STAGES, 8)),
            pltpu.SemaphoreType.DMA((4,)),
            pltpu.SemaphoreType.DMA((4,)),
            pltpu.SemaphoreType.DMA((STAGES, 8)),
            pltpu.SemaphoreType.DMA((STAGES, 8)),
            pltpu.SemaphoreType.DMA((4, 3)),
            pltpu.SemaphoreType.DMA((4, 2)),
            pltpu.SemaphoreType.DMA((8,)),
        ],
        compiler_params=pltpu.CompilerParams(
            collective_id=0, has_side_effects=True, vmem_limit_bytes=60 * 1024 * 1024
        ),
        cost_estimate=pl.CostEstimate(
            flops=4 * 4 * 768 * 2048 * 128, bytes_accessed=8 << 20, transcendentals=4 * 768 * 2048
        ),
    )(
        hist_blocks,
        ranker_list,
        owner_ids,
        slot_ids,
        block_mask,
        queries.reshape(queries.shape[2:]),
        gates.reshape(rows, H * DH),
        tokens.reshape(rows, H * DH),
        w_out,
        norm_gain.reshape(1, H * DH),
        kv_cache,
    )
    return mixed.reshape(tokens.shape)


def solution(mesh):
    fused = mesh.shape["cuts"] == CUTS and mesh.shape["dev"] == DEVS
    local = local_fused if fused else local_general
    return jax.shard_map(
        local,
        mesh=mesh,
        in_specs=(
            P(("cuts", "dev"), None, None),
            P("cuts", "dev", None, None),
            P("cuts", None, "dev", None),
            P("cuts", None, "dev", None),
            P("dev", None),
            P(),
            P(),
            P(),
            P(),
            P(),
            P(),
        ),
        out_specs=P("cuts", None, "dev", None),
        check_vma=False,
    )
```

```python
import functools

import jax
import jax.numpy as jnp
from jax import lax
from jax.experimental import pallas as pl
from jax.experimental.pallas import tpu as pltpu
from jax.sharding import PartitionSpec as P

H = 8
DH = 128
HB = 32
RQ = 4
TILE = 32


EPS = 1e-05


def ranked(selected, count):
    sequence = jnp.cumsum(selected.astype(jnp.int32), axis=-1) - 1
    picks = jnp.arange(count, dtype=jnp.int32)
    return selected[..., None, :] & (sequence[..., None, :] == picks[:, None])


def local_general(
    kv_cache,
    queries,
    gates,
    tokens,
    w_out,
    norm_gain,
    hist_blocks,
    ranker_list,
    owner_ids,
    slot_ids,
    block_mask,
):
    cut_count = lax.axis_size("cuts")
    dev_count = lax.axis_size("dev")
    this_cut = lax.axis_index("cuts")
    this_dev = lax.axis_index("dev")
    groups = dev_count // H
    group_index = this_dev % groups
    pool_size, block_items, width = kv_cache.shape
    slab_width = width // H
    head_size = slab_width // 2
    owned = pool_size // cut_count
    per_group = RQ * HB
    live_cut = owned * cut_count * dev_count
    capacity = (min(per_group, live_cut) + dev_count - 1) // dev_count
    request_count = ranker_list.shape[1]
    keys_cut = request_count * HB
    cut_rows = jnp.arange(cut_count)[:, None]
    owners_ranked = owner_ids[cut_rows, ranker_list].reshape(cut_count, keys_cut)
    slots_ranked = slot_ids[cut_rows, ranker_list].reshape(cut_count, keys_cut)
    owner_self = this_cut * dev_count + this_dev
    chosen = ranked(owners_ranked == owner_self, owned)
    send_rows = jnp.sum(jnp.where(chosen, slots_ranked[:, None, :], 0), axis=-1)
    packed = kv_cache[send_rows.reshape(-1)].reshape(cut_count, owned, block_items, width)
    arrived = lax.all_to_all(packed, "cuts", split_axis=0, concat_axis=0, tiled=True)
    owner_table = lax.dynamic_index_in_dim(owners_ranked, this_cut, 0, keepdims=False)
    sources = jnp.arange(cut_count, dtype=jnp.int32) * dev_count + this_dev
    relay_pick = ranked(owner_table[None, :] == sources[:, None], owned)
    key_index = jnp.arange(keys_cut, dtype=jnp.int32)
    key_of = jnp.sum(jnp.where(relay_pick, key_index, 0), axis=-1).reshape(pool_size)
    group_of = key_of // per_group
    sequence = jnp.arange(pool_size)
    earlier = (group_of[None, :] == group_of[:, None]) & (sequence[None, :] < sequence[:, None])
    target = group_of * capacity + jnp.sum(earlier, axis=1)
    heads_first = arrived.reshape(pool_size, block_items, H, slab_width).transpose(2, 0, 1, 3)
    outgoing = jnp.zeros((H, groups * capacity, block_items, slab_width), arrived.dtype)
    outgoing = (
        outgoing.at[:, target]
        .set(heads_first)
        .reshape(dev_count, capacity, block_items, slab_width)
    )
    received = lax.all_to_all(outgoing, "dev", split_axis=0, concat_axis=0, tiled=True)
    flat_blocks = received.reshape(dev_count * capacity, block_items, slab_width)
    cut_list = lax.dynamic_index_in_dim(ranker_list, this_cut, 0, keepdims=False)
    requests = lax.dynamic_slice_in_dim(cut_list, group_index * RQ, RQ)
    lengths = lax.dynamic_index_in_dim(hist_blocks, this_cut, 0, keepdims=False)[requests]
    group_mask = lax.dynamic_index_in_dim(block_mask, this_cut, 0, keepdims=False)[requests]
    live_blocks = jnp.arange(HB, dtype=jnp.int32)[None, :] < lengths[:, None]
    is_live = live_blocks.reshape(per_group)
    group_owners = lax.dynamic_slice_in_dim(owner_table, group_index * per_group, per_group)
    src_dev = group_owners % dev_count
    src_cut = group_owners // dev_count
    position = jnp.arange(per_group)
    before = (
        is_live[None, :]
        & (src_dev[None, :] == src_dev[:, None])
        & (
            (src_cut[None, :] < src_cut[:, None])
            | (src_cut[None, :] == src_cut[:, None]) & (position[None, :] < position[:, None])
        )
    )
    slot_of = jnp.where(is_live, src_dev * capacity + jnp.sum(before, axis=1), 0).reshape(RQ, HB)
    tile_mask = (group_mask * live_blocks[:, None, :].astype(jnp.int32)).astype(jnp.float32)
    query_all = queries.reshape(RQ, -1, head_size)

    def attend(query, slot_rows, tiles):
        blocks = flat_blocks[slot_rows]
        key_rows = blocks[:, :, :head_size].reshape(-1, head_size)
        value_rows = blocks[:, :, head_size:].reshape(-1, head_size)
        scores = jnp.einsum(
            "ce,ke->ck", query, key_rows, preferred_element_type=jnp.float32
        ) * DH ** (-0.5)
        allowed = jnp.repeat(tiles, TILE, axis=0)
        rows_here = query.shape[0]
        weights = jax.nn.silu(scores).reshape(rows_here, HB, block_items) * allowed[:, :, None]
        weights = weights.reshape(rows_here, -1).astype(jnp.bfloat16)
        return jnp.dot(weights, value_rows, preferred_element_type=jnp.float32).astype(jnp.bfloat16)

    attended = lax.map(
        lambda parts: attend(parts[0], parts[1], parts[2]), (query_all, slot_of, tile_mask)
    )
    rows_each = attended.shape[0] * attended.shape[1] // dev_count
    back = lax.all_to_all(
        attended.reshape(dev_count, rows_each, head_size),
        "dev",
        split_axis=0,
        concat_axis=0,
        tiled=True,
    )
    gathered = back.reshape(H, groups, rows_each, head_size).transpose(1, 2, 0, 3)
    gathered = gathered.reshape(groups * rows_each, H * head_size).astype(jnp.float32)
    row_mean = jnp.mean(gathered, axis=-1, keepdims=True)
    centred = gathered - row_mean
    variance = jnp.mean(centred * centred, axis=-1, keepdims=True)
    normed = centred * lax.rsqrt(variance + EPS) * norm_gain
    gate_rows = gates.reshape(-1, H * head_size).astype(jnp.float32)
    gated = (normed * jax.nn.silu(gate_rows)).astype(jnp.bfloat16)
    projected = jnp.dot(
        gated, lax.all_gather(w_out, "dev", axis=0, tiled=True), preferred_element_type=jnp.float32
    )
    return (tokens.astype(jnp.float32) + projected.reshape(tokens.shape)).astype(jnp.bfloat16)


CUTS = 4
DEVS = 8
STAGES = 4
MESH = pl.DeviceIdType.MESH


def rem(a, b):
    return lax.rem(a, jnp.int32(b))


def div(a, b):
    return lax.div(a, jnp.int32(b))


def fused_kernel(
    hist_ref,
    rank_ref,
    owner_hbm,
    slot_hbm,
    seen_hbm,
    q_hbm,
    gates_hbm,
    tokens_hbm,
    w_hbm,
    gain_hbm,
    kv_hbm,
    out_ref,
    owner_ref,
    slot_ref,
    seen_ref,
    gates_ref,
    tokens_ref,
    gain_ref,
    rows_ref,
    slot_of_ref,
    place_ref,
    mask_ref,
    kv0,
    kv1,
    kv2,
    kv3,
    pk,
    rx,
    qbuf,
    qnow,
    acc,
    ab,
    parts,
    wbuf,
    load_sem,
    kv_send,
    kv_recv,
    q_send,
    q_recv,
    p_send,
    p_recv,
    w_send,
    w_recv,
    table_sem,
):
    loaded = (kv0, kv1, kv2, kv3)
    cut = lax.axis_index("cuts")
    dev = lax.axis_index("dev")
    x, y = rem(cut, 2), div(cut, 2)
    z, core = div(dev, 2), rem(dev, 2)

    def cut_at(off):
        return rem(y + div(off, 2), 2) * 2 + rem(x + rem(off, 2), 2)

    def core_at(off):
        return rem(core + off, 2)

    def load(s, oh):
        head = rem(z + s, 4) * 2 + core_at(oh)
        columns = pl.ds(pl.multiple_of(head * 256, 256), 256)
        return pltpu.make_async_copy(
            kv_hbm.at[:, :, columns], loaded[s].at[oh], load_sem.at[s, oh]
        )

    fetch = [
        pltpu.make_async_copy(source, target, table_sem.at[i])
        for i, (source, target) in enumerate(
            (
                (owner_hbm, owner_ref),
                (slot_hbm, slot_ref),
                (seen_hbm, seen_ref),
                (q_hbm, qbuf.at[0]),
                (w_hbm, wbuf.at[z, 0]),
                (gates_hbm, gates_ref),
                (tokens_hbm, tokens_ref),
                (gain_hbm, gain_ref),
            )
        )
    ]
    for i in (0, 1):
        fetch[i].start()
    for oh in range(2):
        load(0, oh).start()
    for i in (3, 2, 4):
        fetch[i].start()
    for s in range(1, STAGES):
        for oh in range(2):
            load(s, oh).start()
    for i in (5, 6, 7):
        fetch[i].start()

    barrier = pltpu.get_barrier_semaphore()
    for o in range(2, 8):
        pl.semaphore_signal(
            barrier,
            inc=1,
            device_id=(cut_at(o // 2), z * 2 + core_at(o % 2)),
            device_id_type=MESH,
        )
    for o in range(1, 8):
        pl.semaphore_signal(
            barrier,
            inc=1,
            device_id=(cut, rem(z + o // 2, 4) * 2 + core_at(o % 2)),
            device_id_type=MESH,
        )
    position = lax.broadcasted_iota(jnp.int32, (RQ, HB), 0) * HB + lax.broadcasted_iota(
        jnp.int32, (RQ, HB), 1
    )
    for i in (0, 1):
        fetch[i].wait()
    for oc in range(CUTS):
        mine = owner_ref[cut_at(oc)] == cut * DEVS + dev
        coded = position * DEVS + slot_ref[cut_at(oc)]
        rows_ref[oc * 2] = rem(jnp.min(jnp.where(mine, coded, 1 << 20)), DEVS)
        rows_ref[oc * 2 + 1] = rem(jnp.max(jnp.where(mine, coded, 0)), DEVS)
    pl.semaphore_wait(barrier, 13)

    def kv_copy(s, o):
        return pltpu.make_async_remote_copy(
            src_ref=pk.at[s, o],
            dst_ref=rx.at[s, o],
            send_sem=kv_send.at[s, o],
            recv_sem=kv_recv.at[s, o],
            device_id=(cut_at(div(o, 2)), z * 2 + core_at(rem(o, 2))),
            device_id_type=MESH,
        )

    def q_copy(o):
        return pltpu.make_async_remote_copy(
            src_ref=qbuf.at[0],
            dst_ref=qbuf.at[4 - o],
            send_sem=q_send.at[4 - o],
            recv_sem=q_recv.at[4 - o],
            device_id=(cut, rem(z + o, 4) * 2 + core),
            device_id_type=MESH,
        )

    def p_copy(s, o):
        where = rem(z + div(o, 2), 4) * 2 + core_at(rem(o, 2))
        return pltpu.make_async_remote_copy(
            src_ref=ab.at[s, where],
            dst_ref=parts.at[s, o],
            send_sem=p_send.at[s, o],
            recv_sem=p_recv.at[s, o],
            device_id=(cut, where),
            device_id_type=MESH,
        )

    def w_copy(zs, way):
        where = (rem(z + 1, 4) * 2 + core, rem(z + 3, 4) * 2 + core, z * 2 + core_at(1))[way]
        return pltpu.make_async_remote_copy(
            src_ref=wbuf.at[zs, 0],
            dst_ref=wbuf.at[zs, way // 2],
            send_sem=w_send.at[zs, way],
            recv_sem=w_recv.at[zs, way // 2],
            device_id=(cut, where),
            device_id_type=MESH,
        )

    def w_each(d, use):
        for way, zs in ((0, z - d), (1, z + d)):

            @pl.when((zs >= 0) & (zs < 4))
            def _():
                @pl.when((z < 3) if way == 0 else (z > 0))
                def _():
                    use(zs, way)

                if d > 0 or way == 0:
                    use(zs, 2)

    def w_step(d):
        for way, zs in ((0, z - d), (1, z + d)):

            @pl.when((zs >= 0) & (zs < 4))
            def _():
                w_copy(zs, way).wait_recv()

        w_each(d, lambda zs, way: w_copy(zs, way).start())

    def pack(s):
        for oh in range(2):
            load(s, oh).wait()

        def one(i, carry):
            oc = 3 - i
            for j in range(2):
                slot = rows_ref[oc * 2 + j]
                for oh in range(2):
                    pk[s, oc * 2 + oh, j] = loaded[s][oh, slot]
            for oh in range(2):

                @pl.when(oc * 2 + oh > 0)
                def _():
                    kv_copy(s, oc * 2 + oh).start()

            return carry

        lax.fori_loop(jnp.int32(0), jnp.int32(4), one, 0)
        rx[s, 0] = pk[s, 0]

    pack(0)
    fetch[3].wait()
    for o in (3, 2, 1):
        q_copy(o).start()
    pack(1)
    fetch[4].wait()
    w_each(0, lambda zs, way: w_copy(zs, way).start())

    owners = owner_ref[cut]
    for o in range(8):
        theirs = owners == cut_at(o // 2) * DEVS + z * 2 + core_at(o % 2)
        lowest = jnp.min(jnp.where(theirs, position, 1 << 20))
        highest = jnp.max(jnp.where(theirs, position, -1))
        for j, place in enumerate((lowest, highest)):
            n = o * 2 + j
            place_ref[:, n * 128 : n * 128 + 128] = jnp.full((1, 128), place, jnp.int32)
            ranked_at = jnp.int32(0)
            for k in range(1, RQ):
                ranked_at += jnp.where(rank_ref[cut, k] == div(place, HB), k, 0)
            slot_of_ref[n] = jnp.minimum(ranked_at, RQ - 1)
    fetch[2].wait()
    allowed = jnp.zeros((6, 2048), jnp.float32)
    for r in range(RQ):
        seen = seen_ref[cut, :, r, :]
        live = lax.broadcasted_iota(jnp.int32, seen.shape, 1) < hist_ref[cut, r]
        seen = jnp.where(live, seen, 0).astype(jnp.float32).astype(jnp.bfloat16)
        index = lax.broadcasted_iota(jnp.int32, (HB, 2048), 0) + r * HB
        onehot = jnp.where(index == place_ref[...], 1.0, 0.0).astype(jnp.bfloat16)
        allowed += jnp.dot(seen, onehot, preferred_element_type=jnp.float32)
    allowed = allowed * (0.5 * DH ** (-0.5))
    for n in range(16):
        mask_ref[n, 0:6, :] = allowed[:, n * 128 : n * 128 + 128]

    def stage(s, carry):
        @pl.when(s > 0)
        def _():
            q_copy(4 - s).wait_recv()

        acc[...] = jnp.zeros_like(acc)
        qnow[...] = qbuf[s].reshape(RQ, 192, 128)

        def block(o, inner):
            @pl.when(o > 0)
            def _():
                kv_copy(s, o).wait_recv()

            products, factors = [], []
            for j in range(2):
                n = o * 2 + j
                where = slot_of_ref[n]
                scores = lax.dot_general(
                    qnow[where],
                    rx[s, o, j, :, 0:128],
                    (((1,), (1,)), ((), ())),
                    preferred_element_type=jnp.float32,
                )
                half = scores.reshape(6, TILE, 128) * mask_ref[n, 0:6, :][:, None, :]
                weights = (half + half * jnp.tanh(half)).reshape(192, 128)
                products.append(
                    jnp.dot(
                        weights.astype(jnp.bfloat16),
                        rx[s, o, j, :, 128:256],
                        preferred_element_type=jnp.float32,
                    )
                )
                factors.append([jnp.where(where == k, 1.0, 0.0) for k in range(RQ)])
            for k in range(RQ):
                acc[k] += products[0] * factors[0][k] + products[1] * factors[1][k]
            return inner

        lax.fori_loop(jnp.int32(0), jnp.int32(8), block, 0)
        ab[s] = acc[...].reshape(8, 96, 128).astype(jnp.bfloat16)

        def send(o, inner):
            p_copy(s, o).start()
            return inner

        lax.fori_loop(jnp.int32(1), jnp.int32(8), send, 0)
        parts[s, 0] = ab[s, z * 2 + core]

        @pl.when(s == 0)
        def _():
            pack(2)
            w_step(1)

        @pl.when(s == 1)
        def _():
            pack(3)
            w_step(2)

        @pl.when(s == 2)
        def _():
            w_step(3)

        return carry

    lax.fori_loop(jnp.int32(0), jnp.int32(STAGES), stage, 0)

    gate_list, total_list = [], []
    for i in (5, 6, 7):
        fetch[i].wait()
    for pr in range(4):
        for oh in range(2):
            head = rem(z + pr, 4) * 2 + core_at(oh)
            columns = pl.ds(pl.multiple_of(head * 128, 128), 128)
            gate = gates_ref[:, columns].astype(jnp.float32)
            gate_list.append(gate / (1.0 + jnp.exp(-gate)) * gain_ref[:, columns])
    for zs in range(4):
        w_copy(zs, 2).wait_recv()
    for s in range(STAGES):
        for o in range(1, 8):
            p_copy(jnp.int32(s), jnp.int32(o)).wait_recv()
    for pr in range(4):
        for oh in range(2):
            total = parts[pr, oh].astype(jnp.float32)
            for ok in range(1, 4):
                total += parts[(pr + ok) % 4, ok * 2 + oh].astype(jnp.float32)
            total_list.append(total)
    features = float(H * DH)
    mean = jnp.sum(sum(total_list), axis=-1, keepdims=True) / features
    centred = [total - mean for total in total_list]
    squares = sum(part * part for part in centred)
    variance = jnp.sum(squares, axis=-1, keepdims=True) / features
    scale = lax.rsqrt(variance + EPS)
    projected = tokens_ref[...].astype(jnp.float32)
    for pr in range(4):
        zs = rem(z + pr, 4)
        for oh in range(2):
            r = pr * 2 + oh
            gated = (centred[r] * scale * gate_list[r]).astype(jnp.bfloat16)
            projected += jnp.dot(gated, wbuf[zs, oh], preferred_element_type=jnp.float32)
    out_ref[...] = projected.astype(out_ref.dtype)

    for o in (1, 2, 3):
        q_copy(o).wait_send()
    for d in range(4):
        w_each(d, lambda zs, way: w_copy(zs, way).wait_send())

    def drain(i, carry):
        s, o = div(i, 7), rem(i, 7) + 1
        kv_copy(s, o).wait_send()
        p_copy(s, o).wait_send()
        return carry

    lax.fori_loop(jnp.int32(0), jnp.int32(28), drain, 0)


def local_fused(
    kv_cache,
    queries,
    gates,
    tokens,
    w_out,
    norm_gain,
    hist_blocks,
    ranker_list,
    owner_ids,
    slot_ids,
    block_mask,
):
    seen = block_mask.transpose(0, 2, 1, 3)
    rows = gates.shape[2]
    vmem = pl.BlockSpec(memory_space=pltpu.VMEM)
    bf16 = jnp.bfloat16
    mixed = pl.pallas_call(
        fused_kernel,
        out_shape=jax.ShapeDtypeStruct((rows, H * DH), bf16),
        in_specs=[pl.BlockSpec(memory_space=pltpu.SMEM)] * 2
        + [pl.BlockSpec(memory_space=pl.ANY)] * 9,
        out_specs=vmem,
        scratch_shapes=[
            pltpu.VMEM(owner_ids.shape, jnp.int32),
            pltpu.VMEM(slot_ids.shape, jnp.int32),
            pltpu.VMEM(seen.shape, jnp.int32),
            pltpu.VMEM((rows, H * DH), bf16),
            pltpu.VMEM((rows, H * DH), bf16),
            pltpu.VMEM((1, H * DH), jnp.float32),
            pltpu.SMEM((8,), jnp.int32),
            pltpu.SMEM((16,), jnp.int32),
            pltpu.VMEM((1, 2048), jnp.int32),
            pltpu.VMEM((16, 8, 128), jnp.float32),
            pltpu.VMEM((2, 8, 128, 256), bf16),
            pltpu.VMEM((2, 8, 128, 256), bf16),
            pltpu.VMEM((2, 8, 128, 256), bf16),
            pltpu.VMEM((2, 8, 128, 256), bf16),
            pltpu.VMEM((STAGES, 8, 2, 128, 256), bf16),
            pltpu.VMEM((STAGES, 8, 2, 128, 256), bf16),
            pltpu.VMEM((STAGES, 768, 128), bf16),
            pltpu.VMEM((RQ, 192, 128), bf16),
            pltpu.VMEM((RQ, 192, 128), jnp.float32),
            pltpu.VMEM((STAGES, 8, 96, 128), bf16),
            pltpu.VMEM((STAGES, 8, 96, 128), bf16),
            pltpu.VMEM((4, 2, 128, 1024), bf16),
            pltpu.SemaphoreType.DMA((STAGES, 2)),
            pltpu.SemaphoreType.DMA((STAGES, 8)),
            pltpu.SemaphoreType.DMA((STAGES, 8)),
            pltpu.SemaphoreType.DMA((4,)),
            pltpu.SemaphoreType.DMA((4,)),
            pltpu.SemaphoreType.DMA((STAGES, 8)),
            pltpu.SemaphoreType.DMA((STAGES, 8)),
            pltpu.SemaphoreType.DMA((4, 3)),
            pltpu.SemaphoreType.DMA((4, 2)),
            pltpu.SemaphoreType.DMA((8,)),
        ],
        compiler_params=pltpu.CompilerParams(
            collective_id=0, has_side_effects=True, vmem_limit_bytes=60 * 1024 * 1024
        ),
        cost_estimate=pl.CostEstimate(
            flops=4 * 4 * 768 * 2048 * 128, bytes_accessed=8 << 20, transcendentals=4 * 768 * 2048
        ),
    )(
        hist_blocks,
        ranker_list,
        owner_ids,
        slot_ids,
        seen,
        queries.reshape(queries.shape[2:]),
        gates.reshape(rows, H * DH),
        tokens.reshape(rows, H * DH),
        w_out,
        norm_gain.reshape(1, H * DH),
        kv_cache,
    )
    return mixed.reshape(tokens.shape)


def solution(mesh):
    fused = mesh.shape["cuts"] == CUTS and mesh.shape["dev"] == DEVS
    local = local_fused if fused else local_general
    return jax.shard_map(
        local,
        mesh=mesh,
        in_specs=(
            P(("cuts", "dev"), None, None),
            P("cuts", "dev", None, None),
            P("cuts", None, "dev", None),
            P("cuts", None, "dev", None),
            P("dev", None),
            P(),
            P(),
            P(),
            P(),
            P(),
            P(),
        ),
        out_specs=P("cuts", None, "dev", None),
        check_vma=False,
    )
```

```python
import functools

import jax
import jax.numpy as jnp
from jax import lax
from jax.experimental import pallas as pl
from jax.experimental.pallas import tpu as pltpu
from jax.sharding import PartitionSpec as P

H = 8
DH = 128
HB = 32
RQ = 4
TILE = 32


EPS = 1e-05


def ranked(selected, count):
    sequence = jnp.cumsum(selected.astype(jnp.int32), axis=-1) - 1
    picks = jnp.arange(count, dtype=jnp.int32)
    return selected[..., None, :] & (sequence[..., None, :] == picks[:, None])


def local_general(
    kv_cache,
    queries,
    gates,
    tokens,
    w_out,
    norm_gain,
    hist_blocks,
    ranker_list,
    owner_ids,
    slot_ids,
    block_mask,
):
    cut_count = lax.axis_size("cuts")
    dev_count = lax.axis_size("dev")
    this_cut = lax.axis_index("cuts")
    this_dev = lax.axis_index("dev")
    groups = dev_count // H
    group_index = this_dev % groups
    pool_size, block_items, width = kv_cache.shape
    slab_width = width // H
    head_size = slab_width // 2
    owned = pool_size // cut_count
    per_group = RQ * HB
    live_cut = owned * cut_count * dev_count
    capacity = (min(per_group, live_cut) + dev_count - 1) // dev_count
    request_count = ranker_list.shape[1]
    keys_cut = request_count * HB
    cut_rows = jnp.arange(cut_count)[:, None]
    owners_ranked = owner_ids[cut_rows, ranker_list].reshape(cut_count, keys_cut)
    slots_ranked = slot_ids[cut_rows, ranker_list].reshape(cut_count, keys_cut)
    owner_self = this_cut * dev_count + this_dev
    chosen = ranked(owners_ranked == owner_self, owned)
    send_rows = jnp.sum(jnp.where(chosen, slots_ranked[:, None, :], 0), axis=-1)
    packed = kv_cache[send_rows.reshape(-1)].reshape(cut_count, owned, block_items, width)
    arrived = lax.all_to_all(packed, "cuts", split_axis=0, concat_axis=0, tiled=True)
    owner_table = lax.dynamic_index_in_dim(owners_ranked, this_cut, 0, keepdims=False)
    sources = jnp.arange(cut_count, dtype=jnp.int32) * dev_count + this_dev
    relay_pick = ranked(owner_table[None, :] == sources[:, None], owned)
    key_index = jnp.arange(keys_cut, dtype=jnp.int32)
    key_of = jnp.sum(jnp.where(relay_pick, key_index, 0), axis=-1).reshape(pool_size)
    group_of = key_of // per_group
    sequence = jnp.arange(pool_size)
    earlier = (group_of[None, :] == group_of[:, None]) & (sequence[None, :] < sequence[:, None])
    target = group_of * capacity + jnp.sum(earlier, axis=1)
    heads_first = arrived.reshape(pool_size, block_items, H, slab_width).transpose(2, 0, 1, 3)
    outgoing = jnp.zeros((H, groups * capacity, block_items, slab_width), arrived.dtype)
    outgoing = (
        outgoing.at[:, target]
        .set(heads_first)
        .reshape(dev_count, capacity, block_items, slab_width)
    )
    received = lax.all_to_all(outgoing, "dev", split_axis=0, concat_axis=0, tiled=True)
    flat_blocks = received.reshape(dev_count * capacity, block_items, slab_width)
    cut_list = lax.dynamic_index_in_dim(ranker_list, this_cut, 0, keepdims=False)
    requests = lax.dynamic_slice_in_dim(cut_list, group_index * RQ, RQ)
    lengths = lax.dynamic_index_in_dim(hist_blocks, this_cut, 0, keepdims=False)[requests]
    group_mask = lax.dynamic_index_in_dim(block_mask, this_cut, 0, keepdims=False)[requests]
    live_blocks = jnp.arange(HB, dtype=jnp.int32)[None, :] < lengths[:, None]
    is_live = live_blocks.reshape(per_group)
    group_owners = lax.dynamic_slice_in_dim(owner_table, group_index * per_group, per_group)
    src_dev = group_owners % dev_count
    src_cut = group_owners // dev_count
    position = jnp.arange(per_group)
    before = (
        is_live[None, :]
        & (src_dev[None, :] == src_dev[:, None])
        & (
            (src_cut[None, :] < src_cut[:, None])
            | (src_cut[None, :] == src_cut[:, None]) & (position[None, :] < position[:, None])
        )
    )
    slot_of = jnp.where(is_live, src_dev * capacity + jnp.sum(before, axis=1), 0).reshape(RQ, HB)
    tile_mask = (group_mask * live_blocks[:, None, :].astype(jnp.int32)).astype(jnp.float32)
    query_all = queries.reshape(RQ, -1, head_size)

    def attend(query, slot_rows, tiles):
        blocks = flat_blocks[slot_rows]
        key_rows = blocks[:, :, :head_size].reshape(-1, head_size)
        value_rows = blocks[:, :, head_size:].reshape(-1, head_size)
        scores = jnp.einsum(
            "ce,ke->ck", query, key_rows, preferred_element_type=jnp.float32
        ) * DH ** (-0.5)
        allowed = jnp.repeat(tiles, TILE, axis=0)
        rows_here = query.shape[0]
        weights = jax.nn.silu(scores).reshape(rows_here, HB, block_items) * allowed[:, :, None]
        weights = weights.reshape(rows_here, -1).astype(jnp.bfloat16)
        return jnp.dot(weights, value_rows, preferred_element_type=jnp.float32).astype(jnp.bfloat16)

    attended = lax.map(
        lambda parts: attend(parts[0], parts[1], parts[2]), (query_all, slot_of, tile_mask)
    )
    rows_each = attended.shape[0] * attended.shape[1] // dev_count
    back = lax.all_to_all(
        attended.reshape(dev_count, rows_each, head_size),
        "dev",
        split_axis=0,
        concat_axis=0,
        tiled=True,
    )
    gathered = back.reshape(H, groups, rows_each, head_size).transpose(1, 2, 0, 3)
    gathered = gathered.reshape(groups * rows_each, H * head_size).astype(jnp.float32)
    row_mean = jnp.mean(gathered, axis=-1, keepdims=True)
    centred = gathered - row_mean
    variance = jnp.mean(centred * centred, axis=-1, keepdims=True)
    normed = centred * lax.rsqrt(variance + EPS) * norm_gain
    gate_rows = gates.reshape(-1, H * head_size).astype(jnp.float32)
    gated = (normed * jax.nn.silu(gate_rows)).astype(jnp.bfloat16)
    projected = jnp.dot(
        gated, lax.all_gather(w_out, "dev", axis=0, tiled=True), preferred_element_type=jnp.float32
    )
    return (tokens.astype(jnp.float32) + projected.reshape(tokens.shape)).astype(jnp.bfloat16)


CUTS = 4
DEVS = 8
STAGES = 4
MESH = pl.DeviceIdType.MESH


def rem(a, b):
    return lax.rem(a, jnp.int32(b))


def div(a, b):
    return lax.div(a, jnp.int32(b))


def fused_kernel(
    hist_ref,
    rank_ref,
    owner_hbm,
    slot_hbm,
    seen_hbm,
    q_hbm,
    gates_hbm,
    tokens_hbm,
    w_hbm,
    gain_hbm,
    kv_hbm,
    out_ref,
    owner_ref,
    slot_ref,
    seen_ref,
    gates_ref,
    tokens_ref,
    gain_ref,
    rows_ref,
    slot_of_ref,
    place_ref,
    mask_ref,
    kv0,
    kv1,
    kv2,
    kv3,
    pk,
    rx,
    qbuf,
    qnow,
    acc,
    ab,
    parts,
    wbuf,
    load_sem,
    kv_send,
    kv_recv,
    q_send,
    q_recv,
    p_send,
    p_recv,
    w_send,
    w_recv,
    table_sem,
):
    loaded = (kv0, kv1, kv2, kv3)
    cut = lax.axis_index("cuts")
    dev = lax.axis_index("dev")
    x, y = rem(cut, 2), div(cut, 2)
    z, core = div(dev, 2), rem(dev, 2)

    def cut_at(off):
        return rem(y + div(off, 2), 2) * 2 + rem(x + rem(off, 2), 2)

    def core_at(off):
        return rem(core + off, 2)

    def load(s, oh):
        head = rem(z + s, 4) * 2 + core_at(oh)
        columns = pl.ds(pl.multiple_of(head * 256, 256), 256)
        return pltpu.make_async_copy(
            kv_hbm.at[:, :, columns], loaded[s].at[oh], load_sem.at[s, oh]
        )

    fetch = [
        pltpu.make_async_copy(source, target, table_sem.at[i])
        for i, (source, target) in enumerate(
            (
                (owner_hbm, owner_ref),
                (slot_hbm, slot_ref),
                (seen_hbm, seen_ref),
                (q_hbm, qbuf.at[0]),
                (w_hbm, wbuf.at[z, 0]),
                (gates_hbm, gates_ref),
                (tokens_hbm, tokens_ref),
                (gain_hbm, gain_ref),
            )
        )
    ]
    for i in (0, 1):
        fetch[i].start()
    for oh in range(2):
        load(0, oh).start()
    for i in (3, 2, 4):
        fetch[i].start()
    for s in range(1, STAGES):
        for oh in range(2):
            load(s, oh).start()
    for i in (5, 6, 7):
        fetch[i].start()

    barrier = pltpu.get_barrier_semaphore()
    for o in range(2, 8):
        pl.semaphore_signal(
            barrier,
            inc=1,
            device_id=(cut_at(o // 2), z * 2 + core_at(o % 2)),
            device_id_type=MESH,
        )
    for o in range(1, 8):
        pl.semaphore_signal(
            barrier,
            inc=1,
            device_id=(cut, rem(z + o // 2, 4) * 2 + core_at(o % 2)),
            device_id_type=MESH,
        )
    position = lax.broadcasted_iota(jnp.int32, (RQ, HB), 0) * HB + lax.broadcasted_iota(
        jnp.int32, (RQ, HB), 1
    )
    for i in (0, 1):
        fetch[i].wait()
    for oc in range(CUTS):
        mine = owner_ref[cut_at(oc)] == cut * DEVS + dev
        coded = position * DEVS + slot_ref[cut_at(oc)]
        rows_ref[oc * 2] = rem(jnp.min(jnp.where(mine, coded, 1 << 20)), DEVS)
        rows_ref[oc * 2 + 1] = rem(jnp.max(jnp.where(mine, coded, 0)), DEVS)
    pl.semaphore_wait(barrier, 13)

    def kv_copy(s, o):
        return pltpu.make_async_remote_copy(
            src_ref=pk.at[s, o],
            dst_ref=rx.at[s, o],
            send_sem=kv_send.at[s, o],
            recv_sem=kv_recv.at[s, o],
            device_id=(cut_at(div(o, 2)), z * 2 + core_at(rem(o, 2))),
            device_id_type=MESH,
        )

    def q_copy(o):
        return pltpu.make_async_remote_copy(
            src_ref=qbuf.at[0],
            dst_ref=qbuf.at[4 - o],
            send_sem=q_send.at[4 - o],
            recv_sem=q_recv.at[4 - o],
            device_id=(cut, rem(z + o, 4) * 2 + core),
            device_id_type=MESH,
        )

    def p_copy(s, o):
        where = rem(z + div(o, 2), 4) * 2 + core_at(rem(o, 2))
        return pltpu.make_async_remote_copy(
            src_ref=ab.at[s, where],
            dst_ref=parts.at[s, o],
            send_sem=p_send.at[s, o],
            recv_sem=p_recv.at[s, o],
            device_id=(cut, where),
            device_id_type=MESH,
        )

    def w_copy(zs, way):
        where = (rem(z + 1, 4) * 2 + core, rem(z + 3, 4) * 2 + core, z * 2 + core_at(1))[way]
        return pltpu.make_async_remote_copy(
            src_ref=wbuf.at[zs, 0],
            dst_ref=wbuf.at[zs, way // 2],
            send_sem=w_send.at[zs, way],
            recv_sem=w_recv.at[zs, way // 2],
            device_id=(cut, where),
            device_id_type=MESH,
        )

    def w_each(d, use):
        for way, zs in ((0, z - d), (1, z + d)):

            @pl.when((zs >= 0) & (zs < 4))
            def _():
                @pl.when((z < 3) if way == 0 else (z > 0))
                def _():
                    use(zs, way)

                if d > 0 or way == 0:
                    use(zs, 2)

    def w_step(d):
        for way, zs in ((0, z - d), (1, z + d)):

            @pl.when((zs >= 0) & (zs < 4))
            def _():
                w_copy(zs, way).wait_recv()

        w_each(d, lambda zs, way: w_copy(zs, way).start())

    def pack(s, now):
        for oh in range(2):
            load(s, oh).wait()

        def one(i, carry):
            oc = 3 - i
            for j in range(2):
                slot = rows_ref[oc * 2 + j]
                for oh in range(2):
                    pk[s, oc * 2 + oh, j] = loaded[s][oh, slot]
            for oh in range(2):
                if now:

                    @pl.when(oc * 2 + oh > 0)
                    def _():
                        kv_copy(s, oc * 2 + oh).start()

            return carry

        lax.fori_loop(jnp.int32(0), jnp.int32(4), one, 0)
        rx[s, 0] = pk[s, 0]

    pack(0, True)
    fetch[3].wait()
    for o in (3, 2, 1):
        q_copy(o).start()
    pack(1, True)
    fetch[4].wait()
    w_each(0, lambda zs, way: w_copy(zs, way).start())
    pack(2, True)
    pack(3, False)

    owners = owner_ref[cut]
    for o in range(8):
        theirs = owners == cut_at(o // 2) * DEVS + z * 2 + core_at(o % 2)
        lowest = jnp.min(jnp.where(theirs, position, 1 << 20))
        highest = jnp.max(jnp.where(theirs, position, -1))
        for j, place in enumerate((lowest, highest)):
            n = o * 2 + j
            place_ref[:, n * 128 : n * 128 + 128] = jnp.full((1, 128), place, jnp.int32)
            ranked_at = jnp.int32(0)
            for k in range(1, RQ):
                ranked_at += jnp.where(rank_ref[cut, k] == div(place, HB), k, 0)
            slot_of_ref[n] = jnp.minimum(ranked_at, RQ - 1)
    fetch[2].wait()
    allowed = jnp.zeros((6, 2048), jnp.float32)
    for r in range(RQ):
        seen = seen_ref[cut, :, r, :]
        live = lax.broadcasted_iota(jnp.int32, seen.shape, 1) < hist_ref[cut, r]
        seen = jnp.where(live, seen, 0).astype(jnp.float32).astype(jnp.bfloat16)
        index = lax.broadcasted_iota(jnp.int32, (HB, 2048), 0) + r * HB
        onehot = jnp.where(index == place_ref[...], 1.0, 0.0).astype(jnp.bfloat16)
        allowed += jnp.dot(seen, onehot, preferred_element_type=jnp.float32)
    allowed = allowed * (0.5 * DH ** (-0.5))
    for n in range(16):
        mask_ref[n, 0:6, :] = allowed[:, n * 128 : n * 128 + 128]

    def stage(s, carry):
        @pl.when(s > 0)
        def _():
            q_copy(4 - s).wait_recv()

        acc[...] = jnp.zeros_like(acc)
        qnow[...] = qbuf[s].reshape(RQ, 192, 128)

        def block(o, inner):
            @pl.when(o > 0)
            def _():
                kv_copy(s, o).wait_recv()

                @pl.when(s == 0)
                def _():
                    kv_copy(3, o).start()

            products, factors = [], []
            for j in range(2):
                n = o * 2 + j
                where = slot_of_ref[n]
                scores = lax.dot_general(
                    qnow[where],
                    rx[s, o, j, :, 0:128],
                    (((1,), (1,)), ((), ())),
                    preferred_element_type=jnp.float32,
                )
                half = scores.reshape(6, TILE, 128) * mask_ref[n, 0:6, :][:, None, :]
                weights = (half + half * jnp.tanh(half)).reshape(192, 128)
                products.append(
                    jnp.dot(
                        weights.astype(jnp.bfloat16),
                        rx[s, o, j, :, 128:256],
                        preferred_element_type=jnp.float32,
                    )
                )
                factors.append([jnp.where(where == k, 1.0, 0.0) for k in range(RQ)])
            for k in range(RQ):
                acc[k] += products[0] * factors[0][k] + products[1] * factors[1][k]
            return inner

        lax.fori_loop(jnp.int32(0), jnp.int32(8), block, 0)
        ab[s] = acc[...].reshape(8, 96, 128).astype(jnp.bfloat16)

        def send(o, inner):
            p_copy(s, o).start()
            return inner

        lax.fori_loop(jnp.int32(1), jnp.int32(8), send, 0)
        parts[s, 0] = ab[s, z * 2 + core]

        @pl.when(s == 0)
        def _():
            w_step(1)

        @pl.when(s == 1)
        def _():
            w_step(2)

        @pl.when(s == 2)
        def _():
            w_step(3)

        return carry

    lax.fori_loop(jnp.int32(0), jnp.int32(STAGES), stage, 0)

    gate_list, total_list = [], []
    for i in (5, 6, 7):
        fetch[i].wait()
    for pr in range(4):
        for oh in range(2):
            head = rem(z + pr, 4) * 2 + core_at(oh)
            columns = pl.ds(pl.multiple_of(head * 128, 128), 128)
            gate = gates_ref[:, columns].astype(jnp.float32)
            gate_list.append(gate / (1.0 + jnp.exp(-gate)) * gain_ref[:, columns])
    for zs in range(4):
        w_copy(zs, 2).wait_recv()
    for s in range(STAGES):
        for o in range(1, 8):
            p_copy(jnp.int32(s), jnp.int32(o)).wait_recv()
    for pr in range(4):
        for oh in range(2):
            total = parts[pr, oh].astype(jnp.float32)
            for ok in range(1, 4):
                total += parts[(pr + ok) % 4, ok * 2 + oh].astype(jnp.float32)
            total_list.append(total)
    features = float(H * DH)
    mean = jnp.sum(sum(total_list), axis=-1, keepdims=True) / features
    centred = [total - mean for total in total_list]
    squares = sum(part * part for part in centred)
    variance = jnp.sum(squares, axis=-1, keepdims=True) / features
    scale = lax.rsqrt(variance + EPS)
    projected = tokens_ref[...].astype(jnp.float32)
    for pr in range(4):
        zs = rem(z + pr, 4)
        for oh in range(2):
            r = pr * 2 + oh
            gated = (centred[r] * scale * gate_list[r]).astype(jnp.bfloat16)
            projected += jnp.dot(gated, wbuf[zs, oh], preferred_element_type=jnp.float32)
    out_ref[...] = projected.astype(out_ref.dtype)

    for o in (1, 2, 3):
        q_copy(o).wait_send()
    for d in range(4):
        w_each(d, lambda zs, way: w_copy(zs, way).wait_send())

    def drain(i, carry):
        s, o = div(i, 7), rem(i, 7) + 1
        kv_copy(s, o).wait_send()
        p_copy(s, o).wait_send()
        return carry

    lax.fori_loop(jnp.int32(0), jnp.int32(28), drain, 0)


def local_fused(
    kv_cache,
    queries,
    gates,
    tokens,
    w_out,
    norm_gain,
    hist_blocks,
    ranker_list,
    owner_ids,
    slot_ids,
    block_mask,
):
    seen = block_mask.transpose(0, 2, 1, 3)
    rows = gates.shape[2]
    vmem = pl.BlockSpec(memory_space=pltpu.VMEM)
    bf16 = jnp.bfloat16
    mixed = pl.pallas_call(
        fused_kernel,
        out_shape=jax.ShapeDtypeStruct((rows, H * DH), bf16),
        in_specs=[pl.BlockSpec(memory_space=pltpu.SMEM)] * 2
        + [pl.BlockSpec(memory_space=pl.ANY)] * 9,
        out_specs=vmem,
        scratch_shapes=[
            pltpu.VMEM(owner_ids.shape, jnp.int32),
            pltpu.VMEM(slot_ids.shape, jnp.int32),
            pltpu.VMEM(seen.shape, jnp.int32),
            pltpu.VMEM((rows, H * DH), bf16),
            pltpu.VMEM((rows, H * DH), bf16),
            pltpu.VMEM((1, H * DH), jnp.float32),
            pltpu.SMEM((8,), jnp.int32),
            pltpu.SMEM((16,), jnp.int32),
            pltpu.VMEM((1, 2048), jnp.int32),
            pltpu.VMEM((16, 8, 128), jnp.float32),
            pltpu.VMEM((2, 8, 128, 256), bf16),
            pltpu.VMEM((2, 8, 128, 256), bf16),
            pltpu.VMEM((2, 8, 128, 256), bf16),
            pltpu.VMEM((2, 8, 128, 256), bf16),
            pltpu.VMEM((STAGES, 8, 2, 128, 256), bf16),
            pltpu.VMEM((STAGES, 8, 2, 128, 256), bf16),
            pltpu.VMEM((STAGES, 768, 128), bf16),
            pltpu.VMEM((RQ, 192, 128), bf16),
            pltpu.VMEM((RQ, 192, 128), jnp.float32),
            pltpu.VMEM((STAGES, 8, 96, 128), bf16),
            pltpu.VMEM((STAGES, 8, 96, 128), bf16),
            pltpu.VMEM((4, 2, 128, 1024), bf16),
            pltpu.SemaphoreType.DMA((STAGES, 2)),
            pltpu.SemaphoreType.DMA((STAGES, 8)),
            pltpu.SemaphoreType.DMA((STAGES, 8)),
            pltpu.SemaphoreType.DMA((4,)),
            pltpu.SemaphoreType.DMA((4,)),
            pltpu.SemaphoreType.DMA((STAGES, 8)),
            pltpu.SemaphoreType.DMA((STAGES, 8)),
            pltpu.SemaphoreType.DMA((4, 3)),
            pltpu.SemaphoreType.DMA((4, 2)),
            pltpu.SemaphoreType.DMA((8,)),
        ],
        compiler_params=pltpu.CompilerParams(
            collective_id=0, has_side_effects=True, vmem_limit_bytes=60 * 1024 * 1024
        ),
        cost_estimate=pl.CostEstimate(
            flops=4 * 4 * 768 * 2048 * 128, bytes_accessed=8 << 20, transcendentals=4 * 768 * 2048
        ),
    )(
        hist_blocks,
        ranker_list,
        owner_ids,
        slot_ids,
        seen,
        queries.reshape(queries.shape[2:]),
        gates.reshape(rows, H * DH),
        tokens.reshape(rows, H * DH),
        w_out,
        norm_gain.reshape(1, H * DH),
        kv_cache,
    )
    return mixed.reshape(tokens.shape)


def solution(mesh):
    fused = mesh.shape["cuts"] == CUTS and mesh.shape["dev"] == DEVS
    local = local_fused if fused else local_general
    return jax.shard_map(
        local,
        mesh=mesh,
        in_specs=(
            P(("cuts", "dev"), None, None),
            P("cuts", "dev", None, None),
            P("cuts", None, "dev", None),
            P("cuts", None, "dev", None),
            P("dev", None),
            P(),
            P(),
            P(),
            P(),
            P(),
            P(),
        ),
        out_specs=P("cuts", None, "dev", None),
        check_vma=False,
    )
```

```python
import functools

import jax
import jax.numpy as jnp
from jax import lax
from jax.experimental import pallas as pl
from jax.experimental.pallas import tpu as pltpu
from jax.sharding import PartitionSpec as P

H = 8
DH = 128
HB = 32
RQ = 4
TILE = 32


EPS = 1e-05


def ranked(selected, count):
    sequence = jnp.cumsum(selected.astype(jnp.int32), axis=-1) - 1
    picks = jnp.arange(count, dtype=jnp.int32)
    return selected[..., None, :] & (sequence[..., None, :] == picks[:, None])


def local_general(
    kv_cache,
    queries,
    gates,
    tokens,
    w_out,
    norm_gain,
    hist_blocks,
    ranker_list,
    owner_ids,
    slot_ids,
    block_mask,
):
    cut_count = lax.axis_size("cuts")
    dev_count = lax.axis_size("dev")
    this_cut = lax.axis_index("cuts")
    this_dev = lax.axis_index("dev")
    groups = dev_count // H
    group_index = this_dev % groups
    pool_size, block_items, width = kv_cache.shape
    slab_width = width // H
    head_size = slab_width // 2
    owned = pool_size // cut_count
    per_group = RQ * HB
    live_cut = owned * cut_count * dev_count
    capacity = (min(per_group, live_cut) + dev_count - 1) // dev_count
    request_count = ranker_list.shape[1]
    keys_cut = request_count * HB
    cut_rows = jnp.arange(cut_count)[:, None]
    owners_ranked = owner_ids[cut_rows, ranker_list].reshape(cut_count, keys_cut)
    slots_ranked = slot_ids[cut_rows, ranker_list].reshape(cut_count, keys_cut)
    owner_self = this_cut * dev_count + this_dev
    chosen = ranked(owners_ranked == owner_self, owned)
    send_rows = jnp.sum(jnp.where(chosen, slots_ranked[:, None, :], 0), axis=-1)
    packed = kv_cache[send_rows.reshape(-1)].reshape(cut_count, owned, block_items, width)
    arrived = lax.all_to_all(packed, "cuts", split_axis=0, concat_axis=0, tiled=True)
    owner_table = lax.dynamic_index_in_dim(owners_ranked, this_cut, 0, keepdims=False)
    sources = jnp.arange(cut_count, dtype=jnp.int32) * dev_count + this_dev
    relay_pick = ranked(owner_table[None, :] == sources[:, None], owned)
    key_index = jnp.arange(keys_cut, dtype=jnp.int32)
    key_of = jnp.sum(jnp.where(relay_pick, key_index, 0), axis=-1).reshape(pool_size)
    group_of = key_of // per_group
    sequence = jnp.arange(pool_size)
    earlier = (group_of[None, :] == group_of[:, None]) & (sequence[None, :] < sequence[:, None])
    target = group_of * capacity + jnp.sum(earlier, axis=1)
    heads_first = arrived.reshape(pool_size, block_items, H, slab_width).transpose(2, 0, 1, 3)
    outgoing = jnp.zeros((H, groups * capacity, block_items, slab_width), arrived.dtype)
    outgoing = (
        outgoing.at[:, target]
        .set(heads_first)
        .reshape(dev_count, capacity, block_items, slab_width)
    )
    received = lax.all_to_all(outgoing, "dev", split_axis=0, concat_axis=0, tiled=True)
    flat_blocks = received.reshape(dev_count * capacity, block_items, slab_width)
    cut_list = lax.dynamic_index_in_dim(ranker_list, this_cut, 0, keepdims=False)
    requests = lax.dynamic_slice_in_dim(cut_list, group_index * RQ, RQ)
    lengths = lax.dynamic_index_in_dim(hist_blocks, this_cut, 0, keepdims=False)[requests]
    group_mask = lax.dynamic_index_in_dim(block_mask, this_cut, 0, keepdims=False)[requests]
    live_blocks = jnp.arange(HB, dtype=jnp.int32)[None, :] < lengths[:, None]
    is_live = live_blocks.reshape(per_group)
    group_owners = lax.dynamic_slice_in_dim(owner_table, group_index * per_group, per_group)
    src_dev = group_owners % dev_count
    src_cut = group_owners // dev_count
    position = jnp.arange(per_group)
    before = (
        is_live[None, :]
        & (src_dev[None, :] == src_dev[:, None])
        & (
            (src_cut[None, :] < src_cut[:, None])
            | (src_cut[None, :] == src_cut[:, None]) & (position[None, :] < position[:, None])
        )
    )
    slot_of = jnp.where(is_live, src_dev * capacity + jnp.sum(before, axis=1), 0).reshape(RQ, HB)
    tile_mask = (group_mask * live_blocks[:, None, :].astype(jnp.int32)).astype(jnp.float32)
    query_all = queries.reshape(RQ, -1, head_size)

    def attend(query, slot_rows, tiles):
        blocks = flat_blocks[slot_rows]
        key_rows = blocks[:, :, :head_size].reshape(-1, head_size)
        value_rows = blocks[:, :, head_size:].reshape(-1, head_size)
        scores = jnp.einsum(
            "ce,ke->ck", query, key_rows, preferred_element_type=jnp.float32
        ) * DH ** (-0.5)
        allowed = jnp.repeat(tiles, TILE, axis=0)
        rows_here = query.shape[0]
        weights = jax.nn.silu(scores).reshape(rows_here, HB, block_items) * allowed[:, :, None]
        weights = weights.reshape(rows_here, -1).astype(jnp.bfloat16)
        return jnp.dot(weights, value_rows, preferred_element_type=jnp.float32).astype(jnp.bfloat16)

    attended = lax.map(
        lambda parts: attend(parts[0], parts[1], parts[2]), (query_all, slot_of, tile_mask)
    )
    rows_each = attended.shape[0] * attended.shape[1] // dev_count
    back = lax.all_to_all(
        attended.reshape(dev_count, rows_each, head_size),
        "dev",
        split_axis=0,
        concat_axis=0,
        tiled=True,
    )
    gathered = back.reshape(H, groups, rows_each, head_size).transpose(1, 2, 0, 3)
    gathered = gathered.reshape(groups * rows_each, H * head_size).astype(jnp.float32)
    row_mean = jnp.mean(gathered, axis=-1, keepdims=True)
    centred = gathered - row_mean
    variance = jnp.mean(centred * centred, axis=-1, keepdims=True)
    normed = centred * lax.rsqrt(variance + EPS) * norm_gain
    gate_rows = gates.reshape(-1, H * head_size).astype(jnp.float32)
    gated = (normed * jax.nn.silu(gate_rows)).astype(jnp.bfloat16)
    projected = jnp.dot(
        gated, lax.all_gather(w_out, "dev", axis=0, tiled=True), preferred_element_type=jnp.float32
    )
    return (tokens.astype(jnp.float32) + projected.reshape(tokens.shape)).astype(jnp.bfloat16)


CUTS = 4
DEVS = 8
STAGES = 4
MESH = pl.DeviceIdType.MESH


def rem(a, b):
    return lax.rem(a, jnp.int32(b))


def div(a, b):
    return lax.div(a, jnp.int32(b))


def fused_kernel(
    hist_ref,
    rank_ref,
    owner_hbm,
    slot_hbm,
    seen_hbm,
    q_hbm,
    gates_hbm,
    tokens_hbm,
    w_hbm,
    gain_hbm,
    kv_hbm,
    out_ref,
    owner_ref,
    slot_ref,
    seen_ref,
    gates_ref,
    tokens_ref,
    gain_ref,
    rows_ref,
    slot_of_ref,
    place_ref,
    mask_ref,
    kv0,
    kv1,
    kv2,
    kv3,
    pk,
    rx,
    qbuf,
    qnow,
    acc,
    ab,
    parts,
    wbuf,
    load_sem,
    kv_send,
    kv_recv,
    q_send,
    q_recv,
    p_send,
    p_recv,
    w_send,
    w_recv,
    table_sem,
):
    loaded = (kv0, kv1, kv2, kv3)
    cut = lax.axis_index("cuts")
    dev = lax.axis_index("dev")
    x, y = rem(cut, 2), div(cut, 2)
    z, core = div(dev, 2), rem(dev, 2)

    def cut_at(off):
        return rem(y + div(off, 2), 2) * 2 + rem(x + rem(off, 2), 2)

    def core_at(off):
        return rem(core + off, 2)

    def load(s, oh):
        head = rem(z + s, 4) * 2 + core_at(oh)
        columns = pl.ds(pl.multiple_of(head * 256, 256), 256)
        return pltpu.make_async_copy(
            kv_hbm.at[:, :, columns], loaded[s].at[oh], load_sem.at[s, oh]
        )

    fetch = [
        pltpu.make_async_copy(source, target, table_sem.at[i])
        for i, (source, target) in enumerate(
            (
                (owner_hbm, owner_ref),
                (slot_hbm, slot_ref),
                (seen_hbm, seen_ref),
                (q_hbm, qbuf.at[z]),
                (w_hbm, wbuf.at[z, 0]),
                (gates_hbm, gates_ref),
                (tokens_hbm, tokens_ref),
                (gain_hbm, gain_ref),
            )
        )
    ]
    for i in (0, 1):
        fetch[i].start()
    for oh in range(2):
        load(0, oh).start()
    for i in (3, 2, 4):
        fetch[i].start()
    for s in range(1, STAGES):
        for oh in range(2):
            load(s, oh).start()
    for i in (5, 6, 7):
        fetch[i].start()

    barrier = pltpu.get_barrier_semaphore()
    for o in range(2, 8):
        pl.semaphore_signal(
            barrier,
            inc=1,
            device_id=(cut_at(o // 2), z * 2 + core_at(o % 2)),
            device_id_type=MESH,
        )
    for o in range(1, 8):
        pl.semaphore_signal(
            barrier,
            inc=1,
            device_id=(cut, rem(z + o // 2, 4) * 2 + core_at(o % 2)),
            device_id_type=MESH,
        )
    position = lax.broadcasted_iota(jnp.int32, (RQ, HB), 0) * HB + lax.broadcasted_iota(
        jnp.int32, (RQ, HB), 1
    )
    for i in (0, 1):
        fetch[i].wait()
    for oc in range(CUTS):
        mine = owner_ref[cut_at(oc)] == cut * DEVS + dev
        coded = position * DEVS + slot_ref[cut_at(oc)]
        rows_ref[oc * 2] = rem(jnp.min(jnp.where(mine, coded, 1 << 20)), DEVS)
        rows_ref[oc * 2 + 1] = rem(jnp.max(jnp.where(mine, coded, 0)), DEVS)
    pl.semaphore_wait(barrier, 13)

    def kv_copy(s, o):
        return pltpu.make_async_remote_copy(
            src_ref=pk.at[s, o],
            dst_ref=rx.at[s, o],
            send_sem=kv_send.at[s, o],
            recv_sem=kv_recv.at[s, o],
            device_id=(cut_at(div(o, 2)), z * 2 + core_at(rem(o, 2))),
            device_id_type=MESH,
        )

    def q_copy(zs, way):
        return pltpu.make_async_remote_copy(
            src_ref=qbuf.at[zs],
            dst_ref=qbuf.at[zs],
            send_sem=q_send.at[zs, way],
            recv_sem=q_recv.at[zs],
            device_id=(cut, rem(z + 1 + 2 * way, 4) * 2 + core),
            device_id_type=MESH,
        )

    def p_copy(s, o):
        where = rem(z + div(o, 2), 4) * 2 + core_at(rem(o, 2))
        return pltpu.make_async_remote_copy(
            src_ref=ab.at[s, where],
            dst_ref=parts.at[s, o],
            send_sem=p_send.at[s, o],
            recv_sem=p_recv.at[s, o],
            device_id=(cut, where),
            device_id_type=MESH,
        )

    def w_copy(zs, way):
        where = (rem(z + 1, 4) * 2 + core, rem(z + 3, 4) * 2 + core, z * 2 + core_at(1))[way]
        return pltpu.make_async_remote_copy(
            src_ref=wbuf.at[zs, 0],
            dst_ref=wbuf.at[zs, way // 2],
            send_sem=w_send.at[zs, way],
            recv_sem=w_recv.at[zs, way // 2],
            device_id=(cut, where),
            device_id_type=MESH,
        )

    def w_each(d, use, partner=True):
        for way, zs in ((0, z - d), (1, z + d)):

            @pl.when((zs >= 0) & (zs < 4))
            def _():
                @pl.when((z < 3) if way == 0 else (z > 0))
                def _():
                    use(zs, way)

                if partner and (d > 0 or way == 0):
                    use(zs, 2)

    def q_step(d):
        for way, zs in ((0, z - d), (1, z + d)):

            @pl.when((zs >= 0) & (zs < 4))
            def _():
                q_copy(zs, way).wait_recv()

        w_each(d, lambda zs, way: q_copy(zs, way).start(), False)

    def w_step(d):
        for way, zs in ((0, z - d), (1, z + d)):

            @pl.when((zs >= 0) & (zs < 4))
            def _():
                w_copy(zs, way).wait_recv()

        w_each(d, lambda zs, way: w_copy(zs, way).start())

    def pack(s, now):
        for oh in range(2):
            load(s, oh).wait()

        def one(i, carry):
            oc = 3 - i
            for j in range(2):
                slot = rows_ref[oc * 2 + j]
                for oh in range(2):
                    pk[s, oc * 2 + oh, j] = loaded[s][oh, slot]
            for oh in range(2):
                if now:

                    @pl.when(oc * 2 + oh > 0)
                    def _():
                        kv_copy(s, oc * 2 + oh).start()

            return carry

        lax.fori_loop(jnp.int32(0), jnp.int32(4), one, 0)
        rx[s, 0] = pk[s, 0]

    pack(0, True)
    fetch[3].wait()
    w_each(0, lambda zs, way: q_copy(zs, way).start(), False)
    pack(1, True)
    pack(2, False)
    pack(3, False)

    owners = owner_ref[cut]
    for o in range(8):
        theirs = owners == cut_at(o // 2) * DEVS + z * 2 + core_at(o % 2)
        lowest = jnp.min(jnp.where(theirs, position, 1 << 20))
        highest = jnp.max(jnp.where(theirs, position, -1))
        for j, place in enumerate((lowest, highest)):
            n = o * 2 + j
            place_ref[:, n * 128 : n * 128 + 128] = jnp.full((1, 128), place, jnp.int32)
            ranked_at = jnp.int32(0)
            for k in range(1, RQ):
                ranked_at += jnp.where(rank_ref[cut, k] == div(place, HB), k, 0)
            slot_of_ref[n] = jnp.minimum(ranked_at, RQ - 1)
    fetch[2].wait()
    allowed = jnp.zeros((6, 2048), jnp.float32)
    for r in range(RQ):
        seen = seen_ref[cut, :, r, :]
        live = lax.broadcasted_iota(jnp.int32, seen.shape, 1) < hist_ref[cut, r]
        seen = jnp.where(live, seen, 0).astype(jnp.float32).astype(jnp.bfloat16)
        index = lax.broadcasted_iota(jnp.int32, (HB, 2048), 0) + r * HB
        onehot = jnp.where(index == place_ref[...], 1.0, 0.0).astype(jnp.bfloat16)
        allowed += jnp.dot(seen, onehot, preferred_element_type=jnp.float32)
    allowed = allowed * (0.5 * DH ** (-0.5))
    for n in range(16):
        mask_ref[n, 0:6, :] = allowed[:, n * 128 : n * 128 + 128]

    for d in (1, 2):
        q_step(d)
    fetch[4].wait()
    w_each(0, lambda zs, way: w_copy(zs, way).start())
    q_step(3)

    def stage(s, carry):
        acc[...] = jnp.zeros_like(acc)
        qnow[...] = qbuf[rem(z + s, 4)].reshape(RQ, 192, 128)

        def block(o, inner):
            @pl.when(o > 0)
            def _():
                kv_copy(s, o).wait_recv()

                @pl.when(s < 2)
                def _():
                    kv_copy(s + 2, o).start()

            products, factors = [], []
            for j in range(2):
                n = o * 2 + j
                where = slot_of_ref[n]
                scores = lax.dot_general(
                    qnow[where],
                    rx[s, o, j, :, 0:128],
                    (((1,), (1,)), ((), ())),
                    preferred_element_type=jnp.float32,
                )
                half = scores.reshape(6, TILE, 128) * mask_ref[n, 0:6, :][:, None, :]
                weights = (half + half * jnp.tanh(half)).reshape(192, 128)
                products.append(
                    jnp.dot(
                        weights.astype(jnp.bfloat16),
                        rx[s, o, j, :, 128:256],
                        preferred_element_type=jnp.float32,
                    )
                )
                factors.append([jnp.where(where == k, 1.0, 0.0) for k in range(RQ)])
            for k in range(RQ):
                acc[k] += products[0] * factors[0][k] + products[1] * factors[1][k]
            return inner

        lax.fori_loop(jnp.int32(0), jnp.int32(8), block, 0)
        ab[s] = acc[...].reshape(8, 96, 128).astype(jnp.bfloat16)

        def send(o, inner):
            p_copy(s, o).start()
            return inner

        lax.fori_loop(jnp.int32(1), jnp.int32(8), send, 0)
        parts[s, 0] = ab[s, z * 2 + core]

        @pl.when(s == 0)
        def _():
            w_step(1)

        @pl.when(s == 1)
        def _():
            w_step(2)

        @pl.when(s == 2)
        def _():
            w_step(3)

        return carry

    lax.fori_loop(jnp.int32(0), jnp.int32(STAGES), stage, 0)

    gate_list, total_list = [], []
    for i in (5, 6, 7):
        fetch[i].wait()
    for pr in range(4):
        for oh in range(2):
            head = rem(z + pr, 4) * 2 + core_at(oh)
            columns = pl.ds(pl.multiple_of(head * 128, 128), 128)
            gate = gates_ref[:, columns].astype(jnp.float32)
            gate_list.append(gate / (1.0 + jnp.exp(-gate)) * gain_ref[:, columns])
    for zs in range(4):
        w_copy(zs, 2).wait_recv()
    for d in range(4):
        w_each(d, lambda zs, way: q_copy(zs, way).wait_send(), False)
        w_each(d, lambda zs, way: w_copy(zs, way).wait_send())

    def drain(i, carry):
        s, o = div(i, 7), rem(i, 7) + 1
        kv_copy(s, o).wait_send()

        @pl.when(s < 3)
        def _():
            p_copy(s, o).wait_send()
            p_copy(s, o).wait_recv()

        return carry

    lax.fori_loop(jnp.int32(0), jnp.int32(28), drain, 0)
    for pr in range(4):
        for oh in range(2):
            early = [ok for ok in range(4) if (pr + ok) % 4 < 3]
            total = parts[(pr + early[0]) % 4, early[0] * 2 + oh].astype(jnp.float32)
            for ok in early[1:]:
                total += parts[(pr + ok) % 4, ok * 2 + oh].astype(jnp.float32)
            total_list.append(total)
    for o in range(1, 8):
        p_copy(jnp.int32(3), jnp.int32(o)).wait_recv()
    for pr in range(4):
        for oh in range(2):
            late = parts[3, (3 - pr) * 2 + oh].astype(jnp.float32)
            total_list[pr * 2 + oh] += late
    features = float(H * DH)
    mean = jnp.sum(sum(total_list), axis=-1, keepdims=True) / features
    centred = [total - mean for total in total_list]
    squares = sum(part * part for part in centred)
    variance = jnp.sum(squares, axis=-1, keepdims=True) / features
    scale = lax.rsqrt(variance + EPS)
    projected = tokens_ref[...].astype(jnp.float32)
    for pr in range(4):
        zs = rem(z + pr, 4)
        gated = jnp.concatenate(
            [centred[r] * scale * gate_list[r] for r in (pr * 2, pr * 2 + 1)], axis=-1
        ).astype(jnp.bfloat16)
        weight = wbuf[zs].reshape(2 * DH, H * DH)
        projected += jnp.dot(gated, weight, preferred_element_type=jnp.float32)
    out_ref[...] = projected.astype(out_ref.dtype)

    for o in range(1, 8):
        p_copy(jnp.int32(3), jnp.int32(o)).wait_send()


def local_fused(
    kv_cache,
    queries,
    gates,
    tokens,
    w_out,
    norm_gain,
    hist_blocks,
    ranker_list,
    owner_ids,
    slot_ids,
    block_mask,
):
    seen = block_mask.transpose(0, 2, 1, 3)
    rows = gates.shape[2]
    vmem = pl.BlockSpec(memory_space=pltpu.VMEM)
    bf16 = jnp.bfloat16
    mixed = pl.pallas_call(
        fused_kernel,
        out_shape=jax.ShapeDtypeStruct((rows, H * DH), bf16),
        in_specs=[pl.BlockSpec(memory_space=pltpu.SMEM)] * 2
        + [pl.BlockSpec(memory_space=pl.ANY)] * 9,
        out_specs=vmem,
        scratch_shapes=[
            pltpu.VMEM(owner_ids.shape, jnp.int32),
            pltpu.VMEM(slot_ids.shape, jnp.int32),
            pltpu.VMEM(seen.shape, jnp.int32),
            pltpu.VMEM((rows, H * DH), bf16),
            pltpu.VMEM((rows, H * DH), bf16),
            pltpu.VMEM((1, H * DH), jnp.float32),
            pltpu.SMEM((8,), jnp.int32),
            pltpu.SMEM((16,), jnp.int32),
            pltpu.VMEM((1, 2048), jnp.int32),
            pltpu.VMEM((16, 8, 128), jnp.float32),
            pltpu.VMEM((2, 8, 128, 256), bf16),
            pltpu.VMEM((2, 8, 128, 256), bf16),
            pltpu.VMEM((2, 8, 128, 256), bf16),
            pltpu.VMEM((2, 8, 128, 256), bf16),
            pltpu.VMEM((STAGES, 8, 2, 128, 256), bf16),
            pltpu.VMEM((STAGES, 8, 2, 128, 256), bf16),
            pltpu.VMEM((STAGES, 768, 128), bf16),
            pltpu.VMEM((RQ, 192, 128), bf16),
            pltpu.VMEM((RQ, 192, 128), jnp.float32),
            pltpu.VMEM((STAGES, 8, 96, 128), bf16),
            pltpu.VMEM((STAGES, 8, 96, 128), bf16),
            pltpu.VMEM((4, 2, 128, 1024), bf16),
            pltpu.SemaphoreType.DMA((STAGES, 2)),
            pltpu.SemaphoreType.DMA((STAGES, 8)),
            pltpu.SemaphoreType.DMA((STAGES, 8)),
            pltpu.SemaphoreType.DMA((4, 2)),
            pltpu.SemaphoreType.DMA((4,)),
            pltpu.SemaphoreType.DMA((STAGES, 8)),
            pltpu.SemaphoreType.DMA((STAGES, 8)),
            pltpu.SemaphoreType.DMA((4, 3)),
            pltpu.SemaphoreType.DMA((4, 2)),
            pltpu.SemaphoreType.DMA((8,)),
        ],
        compiler_params=pltpu.CompilerParams(
            collective_id=0, has_side_effects=True, vmem_limit_bytes=60 * 1024 * 1024
        ),
        cost_estimate=pl.CostEstimate(
            flops=4 * 4 * 768 * 2048 * 128, bytes_accessed=8 << 20, transcendentals=4 * 768 * 2048
        ),
    )(
        hist_blocks,
        ranker_list,
        owner_ids,
        slot_ids,
        seen,
        queries.reshape(queries.shape[2:]),
        gates.reshape(rows, H * DH),
        tokens.reshape(rows, H * DH),
        w_out,
        norm_gain.reshape(1, H * DH),
        kv_cache,
    )
    return mixed.reshape(tokens.shape)


def solution(mesh):
    fused = mesh.shape["cuts"] == CUTS and mesh.shape["dev"] == DEVS
    local = local_fused if fused else local_general
    return jax.shard_map(
        local,
        mesh=mesh,
        in_specs=(
            P(("cuts", "dev"), None, None),
            P("cuts", "dev", None, None),
            P("cuts", None, "dev", None),
            P("cuts", None, "dev", None),
            P("dev", None),
            P(),
            P(),
            P(),
            P(),
            P(),
            P(),
        ),
        out_specs=P("cuts", None, "dev", None),
        check_vma=False,
    )
```

```python
import functools

import jax
import jax.numpy as jnp
from jax import lax
from jax.experimental import pallas as pl
from jax.experimental.pallas import tpu as pltpu
from jax.sharding import PartitionSpec as P

H = 8
DH = 128
HB = 32
RQ = 4
TILE = 32


EPS = 1e-05


def ranked(selected, count):
    sequence = jnp.cumsum(selected.astype(jnp.int32), axis=-1) - 1
    picks = jnp.arange(count, dtype=jnp.int32)
    return selected[..., None, :] & (sequence[..., None, :] == picks[:, None])


def local_general(
    kv_cache,
    queries,
    gates,
    tokens,
    w_out,
    norm_gain,
    hist_blocks,
    ranker_list,
    owner_ids,
    slot_ids,
    block_mask,
):
    cut_count = lax.axis_size("cuts")
    dev_count = lax.axis_size("dev")
    this_cut = lax.axis_index("cuts")
    this_dev = lax.axis_index("dev")
    groups = dev_count // H
    group_index = this_dev % groups
    pool_size, block_items, width = kv_cache.shape
    slab_width = width // H
    head_size = slab_width // 2
    owned = pool_size // cut_count
    per_group = RQ * HB
    live_cut = owned * cut_count * dev_count
    capacity = (min(per_group, live_cut) + dev_count - 1) // dev_count
    request_count = ranker_list.shape[1]
    keys_cut = request_count * HB
    cut_rows = jnp.arange(cut_count)[:, None]
    owners_ranked = owner_ids[cut_rows, ranker_list].reshape(cut_count, keys_cut)
    slots_ranked = slot_ids[cut_rows, ranker_list].reshape(cut_count, keys_cut)
    owner_self = this_cut * dev_count + this_dev
    chosen = ranked(owners_ranked == owner_self, owned)
    send_rows = jnp.sum(jnp.where(chosen, slots_ranked[:, None, :], 0), axis=-1)
    packed = kv_cache[send_rows.reshape(-1)].reshape(cut_count, owned, block_items, width)
    arrived = lax.all_to_all(packed, "cuts", split_axis=0, concat_axis=0, tiled=True)
    owner_table = lax.dynamic_index_in_dim(owners_ranked, this_cut, 0, keepdims=False)
    sources = jnp.arange(cut_count, dtype=jnp.int32) * dev_count + this_dev
    relay_pick = ranked(owner_table[None, :] == sources[:, None], owned)
    key_index = jnp.arange(keys_cut, dtype=jnp.int32)
    key_of = jnp.sum(jnp.where(relay_pick, key_index, 0), axis=-1).reshape(pool_size)
    group_of = key_of // per_group
    sequence = jnp.arange(pool_size)
    earlier = (group_of[None, :] == group_of[:, None]) & (sequence[None, :] < sequence[:, None])
    target = group_of * capacity + jnp.sum(earlier, axis=1)
    heads_first = arrived.reshape(pool_size, block_items, H, slab_width).transpose(2, 0, 1, 3)
    outgoing = jnp.zeros((H, groups * capacity, block_items, slab_width), arrived.dtype)
    outgoing = (
        outgoing.at[:, target]
        .set(heads_first)
        .reshape(dev_count, capacity, block_items, slab_width)
    )
    received = lax.all_to_all(outgoing, "dev", split_axis=0, concat_axis=0, tiled=True)
    flat_blocks = received.reshape(dev_count * capacity, block_items, slab_width)
    cut_list = lax.dynamic_index_in_dim(ranker_list, this_cut, 0, keepdims=False)
    requests = lax.dynamic_slice_in_dim(cut_list, group_index * RQ, RQ)
    lengths = lax.dynamic_index_in_dim(hist_blocks, this_cut, 0, keepdims=False)[requests]
    group_mask = lax.dynamic_index_in_dim(block_mask, this_cut, 0, keepdims=False)[requests]
    live_blocks = jnp.arange(HB, dtype=jnp.int32)[None, :] < lengths[:, None]
    is_live = live_blocks.reshape(per_group)
    group_owners = lax.dynamic_slice_in_dim(owner_table, group_index * per_group, per_group)
    src_dev = group_owners % dev_count
    src_cut = group_owners // dev_count
    position = jnp.arange(per_group)
    before = (
        is_live[None, :]
        & (src_dev[None, :] == src_dev[:, None])
        & (
            (src_cut[None, :] < src_cut[:, None])
            | (src_cut[None, :] == src_cut[:, None]) & (position[None, :] < position[:, None])
        )
    )
    slot_of = jnp.where(is_live, src_dev * capacity + jnp.sum(before, axis=1), 0).reshape(RQ, HB)
    tile_mask = (group_mask * live_blocks[:, None, :].astype(jnp.int32)).astype(jnp.float32)
    query_all = queries.reshape(RQ, -1, head_size)

    def attend(query, slot_rows, tiles):
        blocks = flat_blocks[slot_rows]
        key_rows = blocks[:, :, :head_size].reshape(-1, head_size)
        value_rows = blocks[:, :, head_size:].reshape(-1, head_size)
        scores = jnp.einsum(
            "ce,ke->ck", query, key_rows, preferred_element_type=jnp.float32
        ) * DH ** (-0.5)
        allowed = jnp.repeat(tiles, TILE, axis=0)
        rows_here = query.shape[0]
        weights = jax.nn.silu(scores).reshape(rows_here, HB, block_items) * allowed[:, :, None]
        weights = weights.reshape(rows_here, -1).astype(jnp.bfloat16)
        return jnp.dot(weights, value_rows, preferred_element_type=jnp.float32).astype(jnp.bfloat16)

    attended = lax.map(
        lambda parts: attend(parts[0], parts[1], parts[2]), (query_all, slot_of, tile_mask)
    )
    rows_each = attended.shape[0] * attended.shape[1] // dev_count
    back = lax.all_to_all(
        attended.reshape(dev_count, rows_each, head_size),
        "dev",
        split_axis=0,
        concat_axis=0,
        tiled=True,
    )
    gathered = back.reshape(H, groups, rows_each, head_size).transpose(1, 2, 0, 3)
    gathered = gathered.reshape(groups * rows_each, H * head_size).astype(jnp.float32)
    row_mean = jnp.mean(gathered, axis=-1, keepdims=True)
    centred = gathered - row_mean
    variance = jnp.mean(centred * centred, axis=-1, keepdims=True)
    normed = centred * lax.rsqrt(variance + EPS) * norm_gain
    gate_rows = gates.reshape(-1, H * head_size).astype(jnp.float32)
    gated = (normed * jax.nn.silu(gate_rows)).astype(jnp.bfloat16)
    projected = jnp.dot(
        gated, lax.all_gather(w_out, "dev", axis=0, tiled=True), preferred_element_type=jnp.float32
    )
    return (tokens.astype(jnp.float32) + projected.reshape(tokens.shape)).astype(jnp.bfloat16)


CUTS = 4
DEVS = 8
STAGES = 4
MESH = pl.DeviceIdType.MESH


def rem(a, b):
    return lax.rem(a, jnp.int32(b))


def div(a, b):
    return lax.div(a, jnp.int32(b))


def fused_kernel(
    hist_ref,
    rank_ref,
    owner_hbm,
    slot_hbm,
    seen_hbm,
    q_hbm,
    gates_hbm,
    tokens_hbm,
    w_hbm,
    gain_hbm,
    kv_hbm,
    out_ref,
    owner_ref,
    slot_ref,
    seen_ref,
    gates_ref,
    tokens_ref,
    gain_ref,
    rows_ref,
    slot_of_ref,
    place_ref,
    mask_ref,
    kv0,
    kv1,
    kv2,
    kv3,
    pk,
    rx,
    qbuf,
    qnow,
    acc,
    ab,
    parts,
    wbuf,
    load_sem,
    kv_send,
    kv_recv,
    q_send,
    q_recv,
    p_send,
    p_recv,
    w_send,
    w_recv,
    table_sem,
):
    loaded = (kv0, kv1, kv2, kv3)
    cut = lax.axis_index("cuts")
    dev = lax.axis_index("dev")
    x, y = rem(cut, 2), div(cut, 2)
    z, core = div(dev, 2), rem(dev, 2)

    def cut_at(off):
        return rem(y + div(off, 2), 2) * 2 + rem(x + rem(off, 2), 2)

    def core_at(off):
        return rem(core + off, 2)

    def load(s, oh):
        head = rem(z + s, 4) * 2 + core_at(oh)
        columns = pl.ds(pl.multiple_of(head * 256, 256), 256)
        return pltpu.make_async_copy(
            kv_hbm.at[:, :, columns], loaded[s].at[oh], load_sem.at[s, oh]
        )

    fetch = [
        pltpu.make_async_copy(source, target, table_sem.at[i])
        for i, (source, target) in enumerate(
            (
                (owner_hbm, owner_ref),
                (slot_hbm, slot_ref),
                (seen_hbm, seen_ref),
                (q_hbm, qbuf.at[z]),
                (w_hbm, wbuf.at[z, 0]),
                (gates_hbm, gates_ref),
                (tokens_hbm, tokens_ref),
                (gain_hbm, gain_ref),
            )
        )
    ]
    for i in (0, 1):
        fetch[i].start()
    for oh in range(2):
        load(0, oh).start()
    for i in (3, 2, 4):
        fetch[i].start()
    for s in range(1, STAGES):
        for oh in range(2):
            load(s, oh).start()
    for i in (5, 6, 7):
        fetch[i].start()

    barrier = pltpu.get_barrier_semaphore()
    for o in range(2, 8):
        pl.semaphore_signal(
            barrier,
            inc=1,
            device_id=(cut_at(o // 2), z * 2 + core_at(o % 2)),
            device_id_type=MESH,
        )
    for o in range(1, 8):
        pl.semaphore_signal(
            barrier,
            inc=1,
            device_id=(cut, rem(z + o // 2, 4) * 2 + core_at(o % 2)),
            device_id_type=MESH,
        )
    position = lax.broadcasted_iota(jnp.int32, (RQ, HB), 0) * HB + lax.broadcasted_iota(
        jnp.int32, (RQ, HB), 1
    )
    for i in (0, 1):
        fetch[i].wait()
    for oc in range(CUTS):
        mine = owner_ref[cut_at(oc)] == cut * DEVS + dev
        coded = position * DEVS + slot_ref[cut_at(oc)]
        rows_ref[oc * 2] = rem(jnp.min(jnp.where(mine, coded, 1 << 20)), DEVS)
        rows_ref[oc * 2 + 1] = rem(jnp.max(jnp.where(mine, coded, 0)), DEVS)
    pl.semaphore_wait(barrier, 13)

    def kv_copy(s, o):
        return pltpu.make_async_remote_copy(
            src_ref=pk.at[s, o],
            dst_ref=rx.at[s, o],
            send_sem=kv_send.at[s, o],
            recv_sem=kv_recv.at[s, o],
            device_id=(cut_at(div(o, 2)), z * 2 + core_at(rem(o, 2))),
            device_id_type=MESH,
        )

    def q_copy(zs, way):
        return pltpu.make_async_remote_copy(
            src_ref=qbuf.at[zs],
            dst_ref=qbuf.at[zs],
            send_sem=q_send.at[zs, way],
            recv_sem=q_recv.at[zs],
            device_id=(cut, rem(z + 1 + 2 * way, 4) * 2 + core),
            device_id_type=MESH,
        )

    def p_copy(s, o):
        where = rem(z + div(o, 2), 4) * 2 + core_at(rem(o, 2))
        return pltpu.make_async_remote_copy(
            src_ref=ab.at[s, where],
            dst_ref=parts.at[s, o],
            send_sem=p_send.at[s, o],
            recv_sem=p_recv.at[s, o],
            device_id=(cut, where),
            device_id_type=MESH,
        )

    def w_copy(zs, way):
        where = (rem(z + 1, 4) * 2 + core, rem(z + 3, 4) * 2 + core, z * 2 + core_at(1))[way]
        return pltpu.make_async_remote_copy(
            src_ref=wbuf.at[zs, 0],
            dst_ref=wbuf.at[zs, way // 2],
            send_sem=w_send.at[zs, way],
            recv_sem=w_recv.at[zs, way // 2],
            device_id=(cut, where),
            device_id_type=MESH,
        )

    def w_each(d, use, partner=True):
        for way, zs in ((0, z - d), (1, z + d)):

            @pl.when((zs >= 0) & (zs < 4))
            def _():
                @pl.when((z < 3) if way == 0 else (z > 0))
                def _():
                    use(zs, way)

                if partner and (d > 0 or way == 0):
                    use(zs, 2)

    def q_step(d):
        for way, zs in ((0, z - d), (1, z + d)):

            @pl.when((zs >= 0) & (zs < 4))
            def _():
                q_copy(zs, way).wait_recv()

        w_each(d, lambda zs, way: q_copy(zs, way).start(), False)

    def w_step(d):
        for way, zs in ((0, z - d), (1, z + d)):

            @pl.when((zs >= 0) & (zs < 4))
            def _():
                w_copy(zs, way).wait_recv()

        w_each(d, lambda zs, way: w_copy(zs, way).start())

    def pack(s, now):
        for oh in range(2):
            load(s, oh).wait()

        def one(i, carry):
            oc = 3 - i
            for j in range(2):
                slot = rows_ref[oc * 2 + j]
                for oh in range(2):
                    pk[s, oc * 2 + oh, j] = loaded[s][oh, slot]
            for oh in range(2):
                if now:

                    @pl.when(oc * 2 + oh > 0)
                    def _():
                        kv_copy(s, oc * 2 + oh).start()

            return carry

        lax.fori_loop(jnp.int32(0), jnp.int32(4), one, 0)
        rx[s, 0] = pk[s, 0]

    fetch[3].wait()
    w_each(0, lambda zs, way: q_copy(zs, way).start(), False)
    pack(0, True)
    fetch[4].wait()
    w_each(0, lambda zs, way: w_copy(zs, way).start())
    pack(1, True)
    pack(2, False)
    pack(3, False)

    owners = owner_ref[cut]
    for o in range(8):
        theirs = owners == cut_at(o // 2) * DEVS + z * 2 + core_at(o % 2)
        lowest = jnp.min(jnp.where(theirs, position, 1 << 20))
        highest = jnp.max(jnp.where(theirs, position, -1))
        for j, place in enumerate((lowest, highest)):
            n = o * 2 + j
            place_ref[:, n * 128 : n * 128 + 128] = jnp.full((1, 128), place, jnp.int32)
            ranked_at = jnp.int32(0)
            for k in range(1, RQ):
                ranked_at += jnp.where(rank_ref[cut, k] == div(place, HB), k, 0)
            slot_of_ref[n] = jnp.minimum(ranked_at, RQ - 1)
    fetch[2].wait()
    allowed = jnp.zeros((6, 2048), jnp.float32)
    for r in range(RQ):
        seen = seen_ref[cut, :, r, :]
        live = lax.broadcasted_iota(jnp.int32, seen.shape, 1) < hist_ref[cut, r]
        seen = jnp.where(live, seen, 0).astype(jnp.float32).astype(jnp.bfloat16)
        index = lax.broadcasted_iota(jnp.int32, (HB, 2048), 0) + r * HB
        onehot = jnp.where(index == place_ref[...], 1.0, 0.0).astype(jnp.bfloat16)
        allowed += jnp.dot(seen, onehot, preferred_element_type=jnp.float32)
    allowed = allowed * (0.5 * DH ** (-0.5))
    for n in range(16):
        mask_ref[n, 0:6, :] = allowed[:, n * 128 : n * 128 + 128]

    for d in (1, 2):
        q_step(d)
    w_step(1)
    q_step(3)

    def stage(s, carry):
        acc[...] = jnp.zeros_like(acc)
        qnow[...] = qbuf[rem(z + s, 4)].reshape(RQ, 192, 128)

        def block(o, inner):
            @pl.when(o > 0)
            def _():
                kv_copy(s, o).wait_recv()

                @pl.when(s < 2)
                def _():
                    kv_copy(s + 2, o).start()

            products, factors = [], []
            for j in range(2):
                n = o * 2 + j
                where = slot_of_ref[n]
                scores = lax.dot_general(
                    qnow[where],
                    rx[s, o, j, :, 0:128],
                    (((1,), (1,)), ((), ())),
                    preferred_element_type=jnp.float32,
                )
                half = scores.reshape(6, TILE, 128) * mask_ref[n, 0:6, :][:, None, :]
                weights = (half + half * jnp.tanh(half)).reshape(192, 128)
                products.append(
                    jnp.dot(
                        weights.astype(jnp.bfloat16),
                        rx[s, o, j, :, 128:256],
                        preferred_element_type=jnp.float32,
                    )
                )
                factors.append([jnp.where(where == k, 1.0, 0.0) for k in range(RQ)])
            for k in range(RQ):
                acc[k] += products[0] * factors[0][k] + products[1] * factors[1][k]
            return inner

        lax.fori_loop(jnp.int32(0), jnp.int32(8), block, 0)
        ab[s] = acc[...].reshape(8, 96, 128).astype(jnp.bfloat16)

        def send(o, inner):
            p_copy(s, o).start()
            return inner

        lax.fori_loop(jnp.int32(1), jnp.int32(8), send, 0)
        parts[s, 0] = ab[s, z * 2 + core]

        @pl.when(s == 0)
        def _():
            w_step(2)

        @pl.when(s == 1)
        def _():
            w_step(3)

        return carry

    lax.fori_loop(jnp.int32(0), jnp.int32(STAGES), stage, 0)

    gate_list, total_list = [], []
    for i in (5, 6, 7):
        fetch[i].wait()
    for pr in range(4):
        for oh in range(2):
            head = rem(z + pr, 4) * 2 + core_at(oh)
            columns = pl.ds(pl.multiple_of(head * 128, 128), 128)
            gate = gates_ref[:, columns].astype(jnp.float32)
            gate_list.append(gate / (1.0 + jnp.exp(-gate)) * gain_ref[:, columns])
    for zs in range(4):
        w_copy(zs, 2).wait_recv()
    for d in range(4):
        w_each(d, lambda zs, way: q_copy(zs, way).wait_send(), False)
        w_each(d, lambda zs, way: w_copy(zs, way).wait_send())

    def drain(i, carry):
        s, o = div(i, 7), rem(i, 7) + 1
        kv_copy(s, o).wait_send()

        @pl.when(s < 3)
        def _():
            p_copy(s, o).wait_send()
            p_copy(s, o).wait_recv()

        return carry

    lax.fori_loop(jnp.int32(0), jnp.int32(28), drain, 0)
    for pr in range(4):
        for oh in range(2):
            early = [ok for ok in range(4) if (pr + ok) % 4 < 3]
            total = parts[(pr + early[0]) % 4, early[0] * 2 + oh].astype(jnp.float32)
            for ok in early[1:]:
                total += parts[(pr + ok) % 4, ok * 2 + oh].astype(jnp.float32)
            total_list.append(total)
    for o in range(1, 8):
        p_copy(jnp.int32(3), jnp.int32(o)).wait_recv()
    for pr in range(4):
        for oh in range(2):
            late = parts[3, (3 - pr) * 2 + oh].astype(jnp.float32)
            total_list[pr * 2 + oh] += late
    features = float(H * DH)
    mean = jnp.sum(sum(total_list), axis=-1, keepdims=True) / features
    centred = [total - mean for total in total_list]
    squares = sum(part * part for part in centred)
    variance = jnp.sum(squares, axis=-1, keepdims=True) / features
    scale = lax.rsqrt(variance + EPS)
    projected = tokens_ref[...].astype(jnp.float32)
    for pr in range(4):
        zs = rem(z + pr, 4)
        gated = jnp.concatenate(
            [centred[r] * scale * gate_list[r] for r in (pr * 2, pr * 2 + 1)], axis=-1
        ).astype(jnp.bfloat16)
        weight = wbuf[zs].reshape(2 * DH, H * DH)
        projected += jnp.dot(gated, weight, preferred_element_type=jnp.float32)
    out_ref[...] = projected.astype(out_ref.dtype)

    for o in range(1, 8):
        p_copy(jnp.int32(3), jnp.int32(o)).wait_send()


def local_fused(
    kv_cache,
    queries,
    gates,
    tokens,
    w_out,
    norm_gain,
    hist_blocks,
    ranker_list,
    owner_ids,
    slot_ids,
    block_mask,
):
    seen = block_mask.transpose(0, 2, 1, 3)
    rows = gates.shape[2]
    vmem = pl.BlockSpec(memory_space=pltpu.VMEM)
    bf16 = jnp.bfloat16
    mixed = pl.pallas_call(
        fused_kernel,
        out_shape=jax.ShapeDtypeStruct((rows, H * DH), bf16),
        in_specs=[pl.BlockSpec(memory_space=pltpu.SMEM)] * 2
        + [pl.BlockSpec(memory_space=pl.ANY)] * 9,
        out_specs=vmem,
        scratch_shapes=[
            pltpu.VMEM(owner_ids.shape, jnp.int32),
            pltpu.VMEM(slot_ids.shape, jnp.int32),
            pltpu.VMEM(seen.shape, jnp.int32),
            pltpu.VMEM((rows, H * DH), bf16),
            pltpu.VMEM((rows, H * DH), bf16),
            pltpu.VMEM((1, H * DH), jnp.float32),
            pltpu.SMEM((8,), jnp.int32),
            pltpu.SMEM((16,), jnp.int32),
            pltpu.VMEM((1, 2048), jnp.int32),
            pltpu.VMEM((16, 8, 128), jnp.float32),
            pltpu.VMEM((2, 8, 128, 256), bf16),
            pltpu.VMEM((2, 8, 128, 256), bf16),
            pltpu.VMEM((2, 8, 128, 256), bf16),
            pltpu.VMEM((2, 8, 128, 256), bf16),
            pltpu.VMEM((STAGES, 8, 2, 128, 256), bf16),
            pltpu.VMEM((STAGES, 8, 2, 128, 256), bf16),
            pltpu.VMEM((STAGES, 768, 128), bf16),
            pltpu.VMEM((RQ, 192, 128), bf16),
            pltpu.VMEM((RQ, 192, 128), jnp.float32),
            pltpu.VMEM((STAGES, 8, 96, 128), bf16),
            pltpu.VMEM((STAGES, 8, 96, 128), bf16),
            pltpu.VMEM((4, 2, 128, 1024), bf16),
            pltpu.SemaphoreType.DMA((STAGES, 2)),
            pltpu.SemaphoreType.DMA((STAGES, 8)),
            pltpu.SemaphoreType.DMA((STAGES, 8)),
            pltpu.SemaphoreType.DMA((4, 2)),
            pltpu.SemaphoreType.DMA((4,)),
            pltpu.SemaphoreType.DMA((STAGES, 8)),
            pltpu.SemaphoreType.DMA((STAGES, 8)),
            pltpu.SemaphoreType.DMA((4, 3)),
            pltpu.SemaphoreType.DMA((4, 2)),
            pltpu.SemaphoreType.DMA((8,)),
        ],
        compiler_params=pltpu.CompilerParams(
            collective_id=0, has_side_effects=True, vmem_limit_bytes=60 * 1024 * 1024
        ),
        cost_estimate=pl.CostEstimate(
            flops=4 * 4 * 768 * 2048 * 128, bytes_accessed=8 << 20, transcendentals=4 * 768 * 2048
        ),
    )(
        hist_blocks,
        ranker_list,
        owner_ids,
        slot_ids,
        seen,
        queries.reshape(queries.shape[2:]),
        gates.reshape(rows, H * DH),
        tokens.reshape(rows, H * DH),
        w_out,
        norm_gain.reshape(1, H * DH),
        kv_cache,
    )
    return mixed.reshape(tokens.shape)


def solution(mesh):
    fused = mesh.shape["cuts"] == CUTS and mesh.shape["dev"] == DEVS
    local = local_fused if fused else local_general
    return jax.shard_map(
        local,
        mesh=mesh,
        in_specs=(
            P(("cuts", "dev"), None, None),
            P("cuts", "dev", None, None),
            P("cuts", None, "dev", None),
            P("cuts", None, "dev", None),
            P("dev", None),
            P(),
            P(),
            P(),
            P(),
            P(),
            P(),
        ),
        out_specs=P("cuts", None, "dev", None),
        check_vma=False,
    )
```
